32 devices in a mesh: lat: 4 (over x, core), lon: 8 (over z, y).
Axes of the slice: x: 2, y: 2, z: 4, core: 2. Of those that a mesh axis runs over, the one named last changes fastest.
Arguments:
- adjoint_in: float32 [16, 3, 136, 1024], P('lat', None, None, 'lon'), may hold values from -6 to 6
- frac_x: float32 [16, 1024], P('lat', 'lon'), may hold values from 0 to 1
- frac_y: float32 [16, 1024], P('lat', 'lon'), may hold values from 0 to 1
- dep_tile: int32 [16], P('lat'), may hold values from -1 to 0, as said below
- dep_col: int32 [16], P('lat'), may hold values from 0 to 127
- block_inverse: float32 [16, 2, 68, 68], P('lat'), may hold values from -0.25 to 1
- coupling: float32 [16, 1024], P('lat', 'lon'), may hold values from 0.15 to 0.6
Outputs:
- adjoint_out: float32 [16, 3, 136, 1024], P('lat', None, None, 'lon')
The draws below stay inside these ranges and needn't reach their ends.
Inputs may be any that keep to these rules, and one draw needn't show every extreme that they name: dep_tile * 128 + dep_col is the row's departure offset in columns; it equals -128 in some row and 127 in another.
All inputs are finite; a program needn't handle non-finite values.
Results may differ from the reference program's by a relative error of at most 0.0003.
Values sent between devices are 32-bit elements; how exact they have to be, the bound alone decides.
No kernel may reach another device: no remote copies, remote signals or barrier semaphores. Data moves between devices by JAX's collectives and lax.ppermute only.
A program may use at most 64 MiB of HBM per device.

```python
import jax
import jax.numpy as jnp
from jax import lax

TRACERS = 3
LEV = 136
BLOCK = 68
REACH = 1
COLS = 128
NBLK = 2
NLAT = 16
NLON = 1024


def departure_offsets(key):
    offset_limit = REACH * COLS
    drawn_offsets = jax.random.randint(jax.random.fold_in(key, 11), (NLAT,), -offset_limit, offset_limit, dtype=jnp.int32)
    row_order = jax.random.permutation(jax.random.fold_in(key, 12), NLAT)
    drawn_offsets = drawn_offsets.at[row_order[0]].set(-offset_limit)
    drawn_offsets = drawn_offsets.at[row_order[1]].set(offset_limit - 1)
    return drawn_offsets


def draw_dep_tile(key, part):
    return jnp.floor_divide(departure_offsets(key), COLS).astype(jnp.int32)


def draw_dep_col(key, part):
    drawn_offsets = departure_offsets(key)
    return (drawn_offsets - jnp.floor_divide(drawn_offsets, COLS) * COLS).astype(jnp.int32)


def draw_block_inverse(key, part):
    diagonal = jax.random.uniform(jax.random.fold_in(key, 21), (NLAT, NBLK, BLOCK, 1), jnp.float32, 0.5, 1.0)
    spread = jax.random.uniform(jax.random.fold_in(key, 22), (NLAT, NBLK, BLOCK, BLOCK), jnp.float32, -0.25, 0.25)
    on_diagonal = lax.broadcasted_iota(jnp.int32, (NLAT, NBLK, BLOCK, BLOCK), 2) == lax.broadcasted_iota(jnp.int32, (NLAT, NBLK, BLOCK, BLOCK), 3)
    return jnp.where(on_diagonal, diagonal, spread).astype(jnp.float32)


def steps_of(rng, shape, shards, smallest, largest):
    def one(position, shards_of):
        draws = jax.random.uniform(jax.random.fold_in(jax.random.fold_in(rng, 6), position), (shards_of,), jnp.float32, smallest / len(shards), largest / len(shards))
        return jnp.repeat(jnp.exp(draws), shape[position] // shards_of).reshape((-1,) + (1,) * (len(shape) - position - 1))

    loudness = one(*shards[0])
    for cut in shards[1:]:
        loudness = loudness * one(*cut)
    return loudness


def scatter_about(key, extent, width, bound, cuts=(), kind=jnp.bfloat16):
    drawn = jax.random.normal(key, extent, jnp.float32) * width
    if len(cuts) > 0:
        drawn = steps_of(key, extent, cuts, -0.22, 0.18) * drawn
    return jnp.clip(drawn, min=-bound, max=bound).astype(kind)


def setup_inputs(seed: int = 0) -> dict:
    streams_of = jax.random.split(jax.random.key(seed), 8)
    adjoint_in = scatter_about(streams_of[0], (NLAT, TRACERS, LEV, NLON), 1.0, 6.0, ((0, 4), (3, 8)), jnp.float32)
    frac_x = jnp.clip(1.0 * jax.random.uniform(streams_of[1], (NLAT, NLON), jnp.float32) ** steps_of(streams_of[1], (NLAT, NLON), ((0, 4), (1, 8)), -0.2, 0.2), 0.0, 1.0)
    frac_y = jnp.clip(1.0 * jax.random.uniform(streams_of[2], (NLAT, NLON), jnp.float32) ** steps_of(streams_of[2], (NLAT, NLON), ((0, 4), (1, 8)), -0.2, 0.2), 0.0, 1.0)
    dep_tile = draw_dep_tile(jax.random.fold_in(streams_of[7], 71), 0)
    dep_col = draw_dep_col(jax.random.fold_in(streams_of[7], 71), 0)
    block_inverse = draw_block_inverse(jax.random.fold_in(streams_of[7], 71), 0)
    coupling = jnp.clip(0.15 + 0.45000002 * jax.random.uniform(streams_of[6], (NLAT, NLON), jnp.float32) ** steps_of(streams_of[6], (NLAT, NLON), ((0, 4), (1, 8)), -0.2, 0.2), 0.15, 0.6)
    return dict(adjoint_in=adjoint_in, frac_x=frac_x, frac_y=frac_y, dep_tile=dep_tile, dep_col=dep_col, block_inverse=block_inverse, coupling=coupling)


def cubic_weights(fraction):
    plus_one = fraction + 1.0
    minus_one = fraction - 1.0
    minus_two = fraction - 2.0
    return jnp.stack([-fraction * minus_one * minus_two / 6.0, plus_one * minus_one * minus_two / 2.0, -plus_one * fraction * minus_two / 2.0, plus_one * fraction * minus_one / 6.0])


def vertical(field_in, inverse, coupling):
    row_count, tracer_count, level_count, col_count = field_in.shape
    block_count = inverse.shape[1]
    block_size = inverse.shape[2]
    blocks = field_in.reshape(row_count, tracer_count, block_count, block_size, col_count)
    first_sweep = jnp.einsum("rnij,rtnjc->rtnic", inverse, blocks, precision=lax.Precision.HIGHEST)
    coupling_now = coupling[:, None, None, :]
    adjusted = blocks.at[:, :, :-1, block_size - 1, :].add(coupling_now * first_sweep[:, :, 1:, 0, :])
    adjusted = adjusted.at[:, :, 1:, 0, :].add(coupling_now * first_sweep[:, :, :-1, block_size - 1, :])
    second_sweep = jnp.einsum("rnij,rtnjc->rtnic", inverse, adjusted, precision=lax.Precision.HIGHEST)
    return second_sweep.reshape(row_count, tracer_count, level_count, col_count)


def reference(adjoint_in, frac_x, frac_y, dep_tile, dep_col, block_inverse, coupling):
    lat_rows = adjoint_in.shape[0]
    shifts = dep_tile * COLS + dep_col
    weights_x = cubic_weights(frac_x)
    weights_y = cubic_weights(frac_y)

    def one_target(target):
        summed = jnp.zeros(adjoint_in.shape[1:], jnp.float32)
        for a in range(4):
            source = target - a + 1
            inside = jnp.where((source >= 0) & (source < lat_rows), 1.0, 0.0).astype(jnp.float32)
            source_row = jnp.clip(source, 0, lat_rows - 1).astype(jnp.int32)
            values = adjoint_in[source_row]
            for b in range(4):
                factor = weights_y[a, source_row] * weights_x[b, source_row]
                summed = summed + inside * jnp.roll(factor * values, shifts[source_row] + b - 1, axis=2)
        return vertical(summed[None], block_inverse[target][None], coupling[target][None])[0]

    return lax.map(one_target, jnp.arange(lat_rows, dtype=jnp.int32))
```

```python
import functools

import jax
import jax.numpy as jnp
from jax import lax
from jax.experimental import pallas as pl
from jax.experimental.pallas import tpu as pltpu
from jax.sharding import PartitionSpec as P

PIECE = 8
VMEM_BYTES = 48 * 1024 * 1024


def passed_along(x, axis, by):
    devices = lax.axis_size(axis)
    return lax.ppermute(x, axis, [(i, (i + by) % devices) for i in range(devices)])


def shifted(x, axis, by):
    devices = lax.axis_size(axis)
    pairs = [(i, i + by) for i in range(devices) if 0 <= i + by < devices]
    return lax.ppermute(x, axis, pairs)


def wx_weights(f):
    return [
        -f * (f - 1.0) * (f - 2.0) / 6.0,
        (f + 1.0) * (f - 1.0) * (f - 2.0) / 2.0,
        -(f + 1.0) * f * (f - 2.0) / 2.0,
        (f + 1.0) * f * (f - 1.0) / 6.0,
    ]


def plan(tile_ref, col_ref, cols):
    rows = tile_ref.shape[0]
    right_at, left_at = jnp.int32(0), jnp.int32(0)
    entries = []
    for i in range(rows):
        s = tile_ref[i] * cols + col_ref[i]
        right_w = jnp.where(s >= 0, jnp.minimum(s + 2, cols), jnp.where(s == -1, 1, 0))
        left_w = jnp.where(s < 0, jnp.minimum(1 - s, cols), jnp.where(s == 0, 1, 0))
        entries.append((s, right_at, right_w, left_at, left_w))
        right_at = right_at + right_w
        left_at = left_at + left_w
    return entries, right_at, left_at


def pack_kernel(tile_ref, col_ref, x_ref, fx_ref, fy_ref, right_ref, left_ref, far_right_ref, far_left_ref, index_ref, even_ref, odd_ref):
    rows, levels, cols = x_ref.shape
    half = right_ref.shape[1]
    unit = cols // 2
    unit_count = right_ref.shape[0]
    entries, right_total, left_total = plan(tile_ref, col_ref, cols)
    index_ref[0] = ((right_total + unit - 1) // unit) * (unit_count + 1) + (left_total + unit - 1) // unit
    lane = lax.broadcasted_iota(jnp.int32, (half, cols), 1)
    sub8 = lax.broadcasted_iota(jnp.int32, (PIECE, cols), 0)

    for i in range(rows):
        s, right_at, right_w, left_at, left_w = entries[i]

        def lo_hi():
            lo = x_ref[i, 0:half, :]
            tail = jnp.where(sub8 == 0, fx_ref[i : i + 1, :], fy_ref[i : i + 1, :])
            hi = jnp.concatenate([x_ref[i, half:levels, :], tail], axis=0)
            return lo, hi

        def place(dst_ref, first, at, width):
            lo, hi = lo_hi()
            shift = jnp.bitwise_and(at - first, cols - 1)
            lo = pltpu.roll(lo, shift, 1)
            hi = pltpu.roll(hi, shift, 1)
            even_ref[...] = jnp.where(lane < unit, lo, pltpu.roll(hi, unit, 1))
            odd_ref[...] = jnp.where(lane < unit, pltpu.roll(lo, unit, 1), hi)
            window = at // cols
            for k in range(4):
                u = 2 * window + k
                src_ref = even_ref if k % 2 == 0 else odd_ref

                @pl.when((u * unit < at + width) & (u * unit + unit > at))
                def _():
                    uu = jnp.minimum(u, unit_count - 1)
                    place_of = uu * unit + jnp.bitwise_and(lane, unit - 1)
                    mask = (place_of >= at) & (place_of < at + width)
                    dst_ref[uu] = jnp.where(mask, src_ref[...], dst_ref[uu])

        @pl.when(right_w > 0)
        def _():
            place(right_ref, cols - right_w, right_at, right_w)

        @pl.when(left_w > 0)
        def _():
            place(left_ref, jnp.int32(0), left_at, left_w)

        def place_one(dst_ref, column):
            lo, hi = lo_hi()
            lo = pltpu.roll(lo, (i - column) % cols, 1)
            hi = pltpu.roll(hi, (unit + i - column) % cols, 1)
            dst_ref[...] = jnp.where(lane == i, lo, jnp.where(lane == unit + i, hi, dst_ref[...]))

        @pl.when(s == cols - 1)
        def _():
            place_one(far_right_ref, cols - 1)

        @pl.when(s == -cols)
        def _():
            place_one(far_left_ref, 0)


def spread_kernel(tile_ref, col_ref, x_ref, fx_ref, fy_ref, right_ref, left_ref, far_right_ref, far_left_ref, down_ref, mid_ref, up_ref, lo_ref, hi_ref, weight_ref):
    rows, levels, cols = x_ref.shape
    half = right_ref.shape[1]
    unit = cols // 2
    unit_count = right_ref.shape[0]
    entries, _, _ = plan(tile_ref, col_ref, cols)
    lane = lax.broadcasted_iota(jnp.int32, (PIECE, cols), 1)
    lane_big = lax.broadcasted_iota(jnp.int32, (half, cols), 1)
    sub8 = lax.broadcasted_iota(jnp.int32, (PIECE, cols), 0)

    def target(t):
        if t == 0:
            return down_ref, 0
        if t <= rows:
            return mid_ref, t - 1
        return up_ref, t - 1 - rows

    for i in range(rows):
        s, right_at, right_w, left_at, left_w = entries[i]
        goes_right = s >= 0
        at = jnp.where(goes_right, right_at, left_at)
        width = jnp.where(goes_right, right_w, left_w)
        om = jnp.bitwise_and(at, cols - 1)
        window = at // cols

        def units(ref, k):
            return ref[jnp.minimum(2 * window + k, unit_count - 1)]

        def unfold(ref):
            low_lane = jnp.bitwise_and(lane_big, unit - 1)
            even = jnp.where(low_lane >= om, units(ref, 0), units(ref, 2))
            odd = jnp.where(low_lane + unit >= om, units(ref, 1), units(ref, 3))
            lo_ref[...] = jnp.where(lane_big < unit, even, pltpu.roll(odd, unit, 1))
            hi_ref[...] = jnp.where(lane_big < unit, pltpu.roll(even, unit, 1), odd)

        @pl.when(goes_right)
        def _():
            unfold(right_ref)

        @pl.when(jnp.logical_not(goes_right))
        def _():
            unfold(left_ref)

        base = jnp.where(goes_right, s - width, s)
        got_shift = base - at
        cut = jnp.where(goes_right, s, s + cols)
        shifts = [
            (jnp.bitwise_and(got_shift + b - 1, cols - 1), jnp.bitwise_and(s + b - 1, cols - 1))
            for b in range(4)
        ]
        from_got = []
        for b in range(4):
            below = (lane - (b - 1)) < cut
            from_got.append(jnp.where(goes_right, below.astype(jnp.int32), 1 - below.astype(jnp.int32)) != 0)

        def terms(got, home):
            return [
                jnp.where(from_got[b], pltpu.roll(got, shifts[b][0], 1), pltpu.roll(home, shifts[b][1], 1))
                for b in range(4)
            ]

        tail = jnp.where(sub8 == 0, fx_ref[i : i + 1, :], fy_ref[i : i + 1, :])
        fractions = terms(hi_ref[half - PIECE : half, :], tail)
        no_left = (s == -1) | (s == cols - 1)
        no_right = (s == 0) | (s == -cols)
        paired = []
        for b in range(4):
            fx = jnp.broadcast_to(fractions[b][0:1, :], (PIECE, cols))
            fy = jnp.broadcast_to(fractions[b][1:2, :], (PIECE, cols))
            wx = wx_weights(fx)[b]
            if b == 3:
                wx = jnp.where((lane == 0) & no_left, 0.0, wx)
            if b == 0:
                wx = jnp.where((lane == cols - 1) & no_right, 0.0, wx)
            wy = wx_weights(fy)
            paired.append([wx * wy[a] for a in range(4)])

        def add(level, got):
            moved = terms(got, x_ref[i, pl.ds(level, PIECE), :])
            for a in range(4):
                total = moved[0] * paired[0][a]
                for b in range(1, 4):
                    total = total + moved[b] * paired[b][a]
                ref, row = target(i + a)
                if not (a == 3 or i == 0):
                    total = total + ref[row, pl.ds(level, PIECE), :]
                ref[row, pl.ds(level, PIECE), :] = total

        def step(r, carry):
            level = pl.multiple_of(r * PIECE, PIECE)
            add(level, lo_ref[pl.ds(level, PIECE), :])
            add(pl.multiple_of(half + r * PIECE, PIECE), hi_ref[pl.ds(level, PIECE), :])
            return carry

        lax.fori_loop(0, (levels - half) // PIECE, step, 0, unroll=5)
        for level in range(levels - half, half, PIECE):
            add(level, lo_ref[level : level + PIECE, :])

        def add_one(ref_of_unit, place, lane_to, b):
            shift_lo = jnp.bitwise_and(lane_to - place, cols - 1)
            shift_hi = jnp.bitwise_and(lane_to - place - unit, cols - 1)
            tail = pltpu.roll(ref_of_unit(half - PIECE), shift_hi, 1)
            wx = wx_weights(jnp.broadcast_to(tail[0:1, :], (PIECE, cols)))[b]
            wy = wx_weights(jnp.broadcast_to(tail[1:2, :], (PIECE, cols)))
            for a in range(4):
                weight_ref[a] = wx * wy[a]

            def put(level, value):
                for a in range(4):
                    ref, row = target(i + a)
                    old = ref[row, pl.ds(level, PIECE), :]
                    ref[row, pl.ds(level, PIECE), :] = jnp.where(lane == lane_to, old + value * weight_ref[a], old)

            def one(r, carry):
                level = pl.multiple_of(r * PIECE, PIECE)
                value = ref_of_unit(level)
                put(level, pltpu.roll(value, shift_lo, 1))

                @pl.when(level < levels - half)
                def _():
                    put(pl.multiple_of(level + half, PIECE), pltpu.roll(value, shift_hi, 1))

                return carry

            lax.fori_loop(0, half // PIECE, one, 0)

        def in_packed(ref, place):
            u = jnp.minimum(place // unit, unit_count - 1)
            return lambda level: ref[u, pl.ds(level, PIECE), :]

        def in_far(ref):
            return lambda level: ref[pl.ds(level, PIECE), :]

        @pl.when(s == -1)
        def _():
            add_one(in_packed(right_ref, right_at), jnp.bitwise_and(right_at, unit - 1), 0, 3)

        @pl.when(s == cols - 1)
        def _():
            add_one(in_far(far_right_ref), i, 0, 3)

        @pl.when(s == 0)
        def _():
            add_one(in_packed(left_ref, left_at), jnp.bitwise_and(left_at, unit - 1), cols - 1, 0)

        @pl.when(s == -cols)
        def _():
            add_one(in_far(far_left_ref), i, cols - 1, 0)


def vertical_kernel(mid_ref, from_prev_ref, from_next_ref, inverse_ref, coupling_ref, out_ref, matrix_ref):
    rows, tracers, levels, cols = out_ref.shape
    size = inverse_ref.shape[2]
    level_of = lax.broadcasted_iota(jnp.int32, (levels, cols), 0)
    dot = functools.partial(jnp.dot, preferred_element_type=jnp.float32)
    matrix_ref[...] = jnp.zeros(matrix_ref.shape, jnp.float32)
    for i in range(rows):
        matrix_ref[0:size, 0:size] = inverse_ref[i, 0]
        matrix_ref[size:levels, size:levels] = inverse_ref[i, 1]
        matrix = matrix_ref[...]
        m_hi = matrix.astype(jnp.bfloat16)
        m_lo = (matrix - m_hi.astype(jnp.float32)).astype(jnp.bfloat16)
        edge = jnp.where(
            level_of[:, 0:1] < size, matrix[:, size - 1 : size], matrix[:, size : size + 1]
        )
        edge = jnp.broadcast_to(edge, (levels, cols))
        for t in range(tracers):
            field = mid_ref[i, t]
            if i < 2:
                field = field + from_prev_ref[i, t]
            if i == rows - 1:
                field = field + from_next_ref[0, t]
            f_hi = field.astype(jnp.bfloat16)
            f_lo = (field - f_hi.astype(jnp.float32)).astype(jnp.bfloat16)
            first = dot(m_hi, f_hi) + (dot(m_hi, f_lo) + dot(m_lo, f_hi))
            coupling = coupling_ref[i : i + 1, :]
            other = jnp.where(
                level_of < size, coupling * first[size : size + 1, :], coupling * first[size - 1 : size, :]
            )
            out_ref[i, t] = first + edge * other


def on_device(adjoint_in, frac_x, frac_y, dep_tile, dep_col, block_inverse, coupling):
    rows, tracers, levels, cols = adjoint_in.shape
    flat = tracers * levels
    half = (flat + 2 + 2 * PIECE - 1) // (2 * PIECE) * PIECE
    unit_count = 2 * rows
    x = adjoint_in.reshape(rows, flat, cols)
    f32 = jnp.float32
    vmem = pl.BlockSpec(memory_space=pltpu.VMEM)
    smem = pl.BlockSpec(memory_space=pltpu.SMEM)
    params = pltpu.CompilerParams(vmem_limit_bytes=VMEM_BYTES)

    right, left, far_right, far_left, index = pl.pallas_call(
        pack_kernel,
        name="pack",
        out_shape=(
            jax.ShapeDtypeStruct((unit_count, half, cols), f32),
            jax.ShapeDtypeStruct((unit_count, half, cols), f32),
            jax.ShapeDtypeStruct((half, cols), f32),
            jax.ShapeDtypeStruct((half, cols), f32),
            jax.ShapeDtypeStruct((1,), jnp.int32),
        ),
        in_specs=[smem, smem, vmem, vmem, vmem],
        out_specs=(vmem, vmem, vmem, vmem, smem),
        scratch_shapes=[pltpu.VMEM((half, cols), f32), pltpu.VMEM((half, cols), f32)],
        compiler_params=params,
    )(dep_tile, dep_col, x, frac_x, frac_y)

    far_right = passed_along(far_right, "lon", 2)
    far_left = passed_along(far_left, "lon", -2)

    def exchange(right_units, left_units):
        def run(right, left):
            got_right, got_left = right, left
            if right_units:
                got = passed_along(right[:right_units], "lon", 1)
                got_right = lax.dynamic_update_slice(right, got, (0, 0, 0))
            if left_units:
                got = passed_along(left[:left_units], "lon", -1)
                got_left = lax.dynamic_update_slice(left, got, (0, 0, 0))
            return got_right, got_left

        return run

    branches, numbers = [], []
    for r in range(unit_count + 1):
        for l in range(unit_count + 1):
            if r + l <= unit_count + 1:
                numbers.append(len(branches))
                branches.append(exchange(r, l))
            else:
                numbers.append(0)
    r = index[0] // (unit_count + 1)
    l = index[0] % (unit_count + 1)
    starts = [numbers[k * (unit_count + 1)] for k in range(unit_count + 1)]
    which = l
    for k in range(1, unit_count + 1):
        which = which + jnp.where(r >= k, starts[k] - starts[k - 1], 0)
    right, left = lax.switch(which, branches, right, left)

    down, mid, up = pl.pallas_call(
        spread_kernel,
        name="spread",
        out_shape=(
            jax.ShapeDtypeStruct((1, flat, cols), f32),
            jax.ShapeDtypeStruct((rows, flat, cols), f32),
            jax.ShapeDtypeStruct((2, flat, cols), f32),
        ),
        in_specs=[smem, smem, vmem, vmem, vmem, vmem, vmem, vmem, vmem],
        out_specs=(vmem, vmem, vmem),
        scratch_shapes=[
            pltpu.VMEM((half, cols), f32),
            pltpu.VMEM((half, cols), f32),
            pltpu.VMEM((4, PIECE, cols), f32),
        ],
        compiler_params=params,
    )(dep_tile, dep_col, x, frac_x, frac_y, right, left, far_right, far_left)

    from_prev = shifted(up, "lat", 1)
    from_next = shifted(down, "lat", -1)

    return pl.pallas_call(
        vertical_kernel,
        name="vertical",
        out_shape=jax.ShapeDtypeStruct(adjoint_in.shape, f32),
        in_specs=[vmem, vmem, vmem, vmem, vmem],
        out_specs=vmem,
        scratch_shapes=[pltpu.VMEM((levels, levels), f32)],
        compiler_params=params,
    )(
        mid.reshape(rows, tracers, levels, cols),
        from_prev.reshape(2, tracers, levels, cols),
        from_next.reshape(1, tracers, levels, cols),
        block_inverse,
        coupling,
    )


def solution(mesh):
    return jax.shard_map(
        on_device,
        mesh=mesh,
        in_specs=(
            P("lat", None, None, "lon"),
            P("lat", "lon"),
            P("lat", "lon"),
            P("lat"),
            P("lat"),
            P("lat", None, None, None),
            P("lat", "lon"),
        ),
        out_specs=P("lat", None, None, "lon"),
        check_vma=False,
    )
```

```python
import functools

import jax
import jax.numpy as jnp
from jax import lax
from jax.experimental import pallas as pl
from jax.experimental.pallas import tpu as pltpu
from jax.sharding import PartitionSpec as P

PIECE = 8
RIM_UNROLL = 5
MIDDLE_UNROLL = 5
VMEM_BYTES = 48 * 1024 * 1024
PACK_BYTES = 61 * 1024 * 1024


def passed_along(x, axis, by):
    devices = lax.axis_size(axis)
    return lax.ppermute(x, axis, [(i, (i + by) % devices) for i in range(devices)])


def shifted(x, axis, by):
    devices = lax.axis_size(axis)
    pairs = [(i, i + by) for i in range(devices) if 0 <= i + by < devices]
    return lax.ppermute(x, axis, pairs)


def wx_weights(f):
    return [
        -f * (f - 1.0) * (f - 2.0) / 6.0,
        (f + 1.0) * (f - 1.0) * (f - 2.0) / 2.0,
        -(f + 1.0) * f * (f - 2.0) / 2.0,
        (f + 1.0) * f * (f - 1.0) / 6.0,
    ]


def plan(offsets, cols):
    right_at, left_at = jnp.int32(0), jnp.int32(0)
    entries = []
    for s in offsets:
        right_w = jnp.where(s >= 0, jnp.minimum(s + 2, cols), jnp.where(s == -1, 1, 0))
        left_w = jnp.where(s < 0, jnp.minimum(1 - s, cols), jnp.where(s == 0, 1, 0))
        entries.append((s, right_at, right_w, left_at, left_w))
        right_at = right_at + right_w
        left_at = left_at + left_w
    return entries, right_at, left_at


def read_offsets(words_ref, rows, cols):
    words = [words_ref[0, k] for k in range((rows + 3) // 4)]
    return [
        jnp.bitwise_and(lax.shift_right_logical(words[i // 4], 8 * (i % 4)), 2 * cols - 1) - cols
        for i in range(rows)
    ]


def any_of(flags):
    result = flags[0]
    for flag in flags[1:]:
        result = result | flag
    return result


def pack_kernel(
    tile_hbm, col_hbm, x_hbm, fx_hbm, fy_hbm,
    units_ref, far_right_ref, far_left_ref, tail_ref, words_ref, index_ref,
    tile_ref, col_ref, x_ref, fx_ref, fy_ref, small_sems, row_sems,
):
    rows, levels, cols = x_ref.shape
    half = units_ref.shape[1]
    unit = cols // 2
    most = 2 * rows
    room = units_ref.shape[0] // 2
    small = [
        pltpu.make_async_copy(src, dst, small_sems.at[k])
        for k, (src, dst) in enumerate(
            [(tile_hbm, tile_ref), (col_hbm, col_ref), (fx_hbm, fx_ref), (fy_hbm, fy_ref)]
        )
    ]
    for copy in small:
        copy.start()
    big = [pltpu.make_async_copy(x_hbm.at[i], x_ref.at[i], row_sems.at[i]) for i in range(rows)]
    for copy in big:
        copy.start()
    for copy in small:
        copy.wait()
    offsets = [tile_ref[i] * cols + col_ref[i] for i in range(rows)]
    entries, right_total, left_total = plan(offsets, cols)
    r = (right_total + unit - 1) // unit
    l = (left_total + unit - 1) // unit
    first = jnp.where(r == 0, 0, most + 1 + (r - 1) * (most + 2) - (r - 1) * r // 2)
    index_ref[0] = first + l

    lane = lax.broadcasted_iota(jnp.int32, (PIECE, cols), 1)
    low_lane = jnp.bitwise_and(lane, unit - 1)
    low_half = lane < unit
    sub = lax.broadcasted_iota(jnp.int32, (PIECE, cols), 0)
    words = jnp.zeros((PIECE, cols), jnp.int32)
    for k in range((rows + 3) // 4):
        word = jnp.int32(0)
        for i in range(4 * k, min(4 * k + 4, rows)):
            word = word | lax.shift_left(offsets[i] + cols, 8 * (i % 4))
        words = jnp.where(lane == k, word, words)
    words_ref[...] = words
    for i in range(rows):
        tail_ref[i] = jnp.where(sub == 0, fx_ref[i : i + 1, :], fy_ref[i : i + 1, :])

    def place(i, base, start, at, width):
        shift = jnp.bitwise_and(at - start, cols - 1)
        window = at // cols
        masks = []
        for k in range(4):
            place_of = (2 * window + k) * unit + low_lane
            masks.append((place_of >= at) & (place_of < at + width))
        for level in range(0, half, PIECE):
            lo = x_ref[i, level : level + PIECE, :]
            hi = x_ref[i, half + level : half + level + PIECE, :] if half + level < levels else tail_ref[i]
            lo = pltpu.roll(lo, shift, 1)
            hi = pltpu.roll(hi, shift, 1)
            even = jnp.where(low_half, lo, pltpu.roll(hi, unit, 1))
            odd = jnp.where(low_half, pltpu.roll(lo, unit, 1), hi)
            for k in range(4):
                u = base + 2 * window + k
                old = units_ref[u, level : level + PIECE, :]
                units_ref[u, level : level + PIECE, :] = jnp.where(masks[k], odd if k % 2 else even, old)

    for i in range(rows):
        s, right_at, right_w, left_at, left_w = entries[i]
        goes_right = s >= 0
        big[i].wait()
        place(
            i,
            jnp.where(goes_right, 0, room),
            jnp.where(goes_right, cols - right_w, 0),
            jnp.where(goes_right, right_at, left_at),
            jnp.where(goes_right, right_w, left_w),
        )

    def place_far(i, far_ref, column):
        for k in range(2):
            block = far_ref[k * PIECE : (k + 1) * PIECE, :]
            for f in range(half // PIECE):
                level = (2 * f + k) * PIECE
                value = x_ref[i, level : level + PIECE, :] if level < levels else tail_ref[i]
                to = rows * f + i
                block = jnp.where(lane == to, pltpu.roll(value, (to - column) % cols, 1), block)
            far_ref[k * PIECE : (k + 1) * PIECE, :] = block

    @pl.when(any_of([(s == 0) | (s == -1) | (s == cols - 1) | (s == -cols) for s in offsets]))
    def _():
        for i in range(rows):
            s, right_at, right_w, left_at, left_w = entries[i]

            @pl.when((s == 0) | (s == -1))
            def _():
                zero = s == 0
                place(
                    i, jnp.where(zero, room, 0), jnp.where(zero, 0, cols - 1), jnp.where(zero, left_at, right_at), 1
                )

            @pl.when(s == cols - 1)
            def _():
                place_far(i, far_right_ref, cols - 1)

            @pl.when(s == -cols)
            def _():
                place_far(i, far_left_ref, 0)


def spread_kernel(wanted, unroll, words_ref, x_ref, tail_ref, units_ref, far_right_ref, far_left_ref, *refs):
    out_refs, (other_ref, weight_ref) = refs[:-2], refs[-2:]
    rows, levels, cols = x_ref.shape
    half = units_ref.shape[1]
    unit = cols // 2
    room = units_ref.shape[0] // 2
    offsets = read_offsets(words_ref, rows, cols)
    entries, _, _ = plan(offsets, cols)
    lane = lax.broadcasted_iota(jnp.int32, (PIECE, cols), 1)
    low_lane = jnp.bitwise_and(lane, unit - 1)
    low_half = lane < unit
    chosen = sorted({w[0] for w in wanted})

    def fetch_unit(i, u, place, lane_to):
        for level in range(0, half, PIECE):
            value = units_ref[u, level : level + PIECE, :]
            other_ref[i, level : level + PIECE, :] = pltpu.roll(value, jnp.bitwise_and(lane_to - place, cols - 1), 1)
            other_ref[i, half + level : half + level + PIECE, :] = pltpu.roll(
                value, jnp.bitwise_and(lane_to - place - unit, cols - 1), 1
            )

    def fetch_far(i, far_ref, lane_to):
        for k in range(2):
            block = far_ref[k * PIECE : (k + 1) * PIECE, :]
            for f in range(half // PIECE):
                level = (2 * f + k) * PIECE
                other_ref[i, level : level + PIECE, :] = pltpu.roll(block, (lane_to - rows * f - i) % cols, 1)

    @pl.when(any_of([(s == 0) | (s == -1) | (s == cols - 1) | (s == -cols) for s in (offsets[i] for i in chosen)]))
    def _():
        for i in chosen:
            s, right_at, right_w, left_at, left_w = entries[i]

            @pl.when((s == 0) | (s == -1))
            def _():
                zero = s == 0
                place = jnp.where(zero, left_at, right_at)
                u = jnp.where(zero, room, 0) + place // unit
                fetch_unit(i, u, jnp.bitwise_and(place, unit - 1), jnp.where(zero, cols - 1, 0))

            @pl.when(s == cols - 1)
            def _():
                fetch_far(i, far_right_ref, 0)

            @pl.when(s == -cols)
            def _():
                fetch_far(i, far_left_ref, cols - 1)

    made = {}
    for i in chosen:
        s, right_at, right_w, left_at, left_w = entries[i]
        goes_right = s >= 0
        at = jnp.where(goes_right, right_at, left_at)
        width = jnp.where(goes_right, right_w, left_w)
        base = jnp.where(goes_right, 0, room) + 2 * (at // cols)
        om = jnp.bitwise_and(at, cols - 1)
        even_first = low_lane >= om
        odd_first = low_lane + unit >= om
        start = jnp.where(goes_right, s - width, s)
        cut = jnp.where(goes_right, s, s + cols)
        shifts = [
            (jnp.bitwise_and(start - at + b - 1, cols - 1), jnp.bitwise_and(s + b - 1, cols - 1)) for b in range(4)
        ]
        flip = jnp.where(goes_right, 0, 1)
        from_got = [jnp.where((lane - (b - 1)) < cut, 1, 0) != flip for b in range(4)]
        no_left = (s == -1) | (s == cols - 1)
        no_right = (s == 0) | (s == -cols)
        at_left = lane == jnp.where(no_left, 0, -1)
        at_right = lane == jnp.where(no_right, cols - 1, -1)

        def got(level, base=base, even_first=even_first, odd_first=odd_first):
            piece = [units_ref[base + k, pl.ds(level, PIECE), :] for k in range(4)]
            even = jnp.where(even_first, piece[0], piece[2])
            odd = jnp.where(odd_first, piece[1], piece[3])
            lo = jnp.where(low_half, even, pltpu.roll(odd, unit, 1))
            hi = jnp.where(low_half, pltpu.roll(even, unit, 1), odd)
            return lo, hi

        def terms(got, home, other, from_got=from_got, shifts=shifts, at_left=at_left, at_right=at_right):
            moved = [
                jnp.where(from_got[b], pltpu.roll(got, shifts[b][0], 1), pltpu.roll(home, shifts[b][1], 1))
                for b in range(4)
            ]
            moved[0] = jnp.where(at_right, other, moved[0])
            moved[3] = jnp.where(at_left, other, moved[3])
            return moved

        made[i] = (got, terms)

    for i in chosen:
        got, terms = made[i]
        fractions = terms(got(half - PIECE)[1], tail_ref[i], other_ref[i, 2 * half - PIECE : 2 * half, :])
        for b in range(4):
            wx = wx_weights(fractions[b][0:1, :])[b]
            wy = wx_weights(fractions[b][1:2, :])
            for a in range(4):
                weight_ref[i, 4 * a + b : 4 * a + b + 1, :] = wx * wy[a]

    targets = sorted({w[2:] for w in wanted})

    def add(level, values):
        sums = {}
        for i in chosen:
            moved = made[i][1](values[i], x_ref[i, pl.ds(level, PIECE), :], other_ref[i, pl.ds(level, PIECE), :])
            for row, a, out, k in wanted:
                if row == i:
                    for b in range(4):
                        term = moved[b] * weight_ref[i, 4 * a + b : 4 * a + b + 1, :]
                        sums[out, k] = term if (out, k) not in sums else sums[out, k] + term
        for out, k in targets:
            out_refs[out][k, pl.ds(level, PIECE), :] = sums[out, k]

    def step(r, carry):
        level = pl.multiple_of(r * PIECE, PIECE)
        values = {i: made[i][0](level) for i in chosen}
        add(level, {i: values[i][0] for i in chosen})
        add(pl.multiple_of(half + level, PIECE), {i: values[i][1] for i in chosen})
        return carry

    lax.fori_loop(0, (levels - half) // PIECE, step, 0, unroll=unroll)
    for level in range(levels - half, half, PIECE):
        add(level, {i: made[i][0](level)[0] for i in chosen})


def vertical_kernel(mid_ref, from_prev_ref, from_next_ref, inverse_ref, coupling_hbm, out_ref, matrix_ref, coupling_ref, sem):
    rows, tracers, levels, cols = out_ref.shape
    size = inverse_ref.shape[2]
    level_of = lax.broadcasted_iota(jnp.int32, (levels, cols), 0)
    dot = functools.partial(jnp.dot, preferred_element_type=jnp.float32)
    copy = pltpu.make_async_copy(coupling_hbm, coupling_ref, sem)
    copy.start()
    matrix_ref[...] = jnp.zeros(matrix_ref.shape, jnp.float32)
    copy.wait()
    for i in range(rows):
        matrix_ref[0:size, 0:size] = inverse_ref[i, 0]
        matrix_ref[size:levels, size:levels] = inverse_ref[i, 1]
        matrix = matrix_ref[...]
        m_hi = matrix.astype(jnp.bfloat16)
        m_lo = (matrix - m_hi.astype(jnp.float32)).astype(jnp.bfloat16)
        edge = jnp.where(
            level_of[:, 0:1] < size, matrix[:, size - 1 : size], matrix[:, size : size + 1]
        )
        edge = jnp.broadcast_to(edge, (levels, cols))
        for t in range(tracers):
            field = mid_ref[i, t]
            if i < 2:
                field = field + from_prev_ref[i, t]
            if i == rows - 1:
                field = field + from_next_ref[0, t]
            f_hi = field.astype(jnp.bfloat16)
            f_lo = (field - f_hi.astype(jnp.float32)).astype(jnp.bfloat16)
            first = dot(m_hi, f_hi) + (dot(m_hi, f_lo) + dot(m_lo, f_hi))
            coupling = coupling_ref[i : i + 1, :]
            other = jnp.where(
                level_of < size, coupling * first[size : size + 1, :], coupling * first[size - 1 : size, :]
            )
            out_ref[i, t] = first + edge * other


def on_device(adjoint_in, frac_x, frac_y, dep_tile, dep_col, block_inverse, coupling):
    rows, tracers, levels, cols = adjoint_in.shape
    flat = tracers * levels
    half = (flat + 2 + 2 * PIECE - 1) // (2 * PIECE) * PIECE
    most = 2 * rows
    room = most + 4
    x = adjoint_in.reshape(rows, flat, cols)
    f32 = jnp.float32
    vmem = pl.BlockSpec(memory_space=pltpu.VMEM)
    smem = pl.BlockSpec(memory_space=pltpu.SMEM)
    params = pltpu.CompilerParams(vmem_limit_bytes=VMEM_BYTES)

    units, far_right, far_left, tail, words, index = pl.pallas_call(
        pack_kernel,
        name="pack",
        out_shape=(
            jax.ShapeDtypeStruct((2 * room, half, cols), f32),
            jax.ShapeDtypeStruct((2 * PIECE, cols), f32),
            jax.ShapeDtypeStruct((2 * PIECE, cols), f32),
            jax.ShapeDtypeStruct((rows, PIECE, cols), f32),
            jax.ShapeDtypeStruct((PIECE, cols), jnp.int32),
            jax.ShapeDtypeStruct((1,), jnp.int32),
        ),
        in_specs=[pl.BlockSpec(memory_space=pltpu.HBM)] * 5,
        out_specs=(vmem, vmem, vmem, vmem, vmem, smem),
        scratch_shapes=[
            pltpu.SMEM((rows,), jnp.int32),
            pltpu.SMEM((rows,), jnp.int32),
            pltpu.VMEM((rows, flat, cols), f32),
            pltpu.VMEM((rows, cols), f32),
            pltpu.VMEM((rows, cols), f32),
            pltpu.SemaphoreType.DMA((4,)),
            pltpu.SemaphoreType.DMA((rows,)),
        ],
        compiler_params=pltpu.CompilerParams(vmem_limit_bytes=PACK_BYTES),
    )(dep_tile, dep_col, x, frac_x, frac_y)

    def exchange(right_units, left_units):
        def run(units, *far):
            sends, places = [], []
            if right_units:
                sends.append((units[:right_units], 1))
                places.append((0, 0, 0))
            if left_units:
                sends.append((units[room : room + left_units], -1))
                places.append((room, 0, 0))
            sends.append((far[0], 2))
            sends.append((far[1], -2))
            taken = lax.optimization_barrier(tuple(value for value, _ in sends))
            arrived = [passed_along(value, "lon", by) for value, (_, by) in zip(taken, sends)]
            arrived = lax.optimization_barrier(tuple(arrived))
            for place, value in zip(places, arrived):
                units = lax.dynamic_update_slice(units, value, place)
            return units, arrived[-2], arrived[-1]

        return run

    branches = [
        exchange(r, l) for r in range(most + 1) for l in range(most + 1) if r + l <= most + 1
    ]
    units, far_right, far_left = lax.switch(index[0], branches, units, far_right, far_left)

    def spread(name, wanted, sizes, unroll):
        return pl.pallas_call(
            functools.partial(spread_kernel, wanted, unroll),
            name=name,
            out_shape=tuple(jax.ShapeDtypeStruct((n, flat, cols), f32) for n in sizes),
            in_specs=[vmem] * 6,
            out_specs=(vmem,) * len(sizes),
            scratch_shapes=[
                pltpu.VMEM((rows, 2 * half, cols), f32),
                pltpu.VMEM((rows, 16, cols), f32),
            ],
            compiler_params=params,
        )(words, x, tail, units, far_right, far_left)

    rim, middle = [], []
    for i in range(rows):
        for a in range(4):
            t = i + a - 1
            if t < 0:
                rim.append((i, a, 0, 0))
            elif t >= rows:
                rim.append((i, a, 1, t - rows))
            else:
                middle.append((i, a, 0, t))
    down, up = spread("rim", rim, (1, 2), RIM_UNROLL)
    from_prev = shifted(up, "lat", 1)
    from_next = shifted(down, "lat", -1)
    (mid,) = spread("middle", middle, (rows,), MIDDLE_UNROLL)

    return pl.pallas_call(
        vertical_kernel,
        name="vertical",
        out_shape=jax.ShapeDtypeStruct(adjoint_in.shape, f32),
        in_specs=[vmem, vmem, vmem, vmem, pl.BlockSpec(memory_space=pltpu.HBM)],
        out_specs=vmem,
        scratch_shapes=[
            pltpu.VMEM((levels, levels), f32),
            pltpu.VMEM((rows, cols), f32),
            pltpu.SemaphoreType.DMA(()),
        ],
        compiler_params=params,
    )(
        mid.reshape(rows, tracers, levels, cols),
        from_prev.reshape(2, tracers, levels, cols),
        from_next.reshape(1, tracers, levels, cols),
        block_inverse,
        coupling,
    )


def solution(mesh):
    return jax.shard_map(
        on_device,
        mesh=mesh,
        in_specs=(
            P("lat", None, None, "lon"),
            P("lat", "lon"),
            P("lat", "lon"),
            P("lat"),
            P("lat"),
            P("lat", None, None, None),
            P("lat", "lon"),
        ),
        out_specs=P("lat", None, None, "lon"),
        check_vma=False,
    )
```

```python
import functools

import jax
import jax.numpy as jnp
from jax import lax
from jax.experimental import pallas as pl
from jax.experimental.pallas import tpu as pltpu
from jax.sharding import PartitionSpec as P

PIECE = 8
VMEM_BYTES = 48 * 1024 * 1024
PACK_BYTES = 61 * 1024 * 1024


def passed_along(x, axis, by):
    devices = lax.axis_size(axis)
    return lax.ppermute(x, axis, [(i, (i + by) % devices) for i in range(devices)])


def shifted(x, axis, by):
    devices = lax.axis_size(axis)
    pairs = [(i, i + by) for i in range(devices) if 0 <= i + by < devices]
    return lax.ppermute(x, axis, pairs)


def wx_weights(f):
    return [
        -f * (f - 1.0) * (f - 2.0) / 6.0,
        (f + 1.0) * (f - 1.0) * (f - 2.0) / 2.0,
        -(f + 1.0) * f * (f - 2.0) / 2.0,
        (f + 1.0) * f * (f - 1.0) / 6.0,
    ]


def plan(offsets, cols):
    right_at, left_at = jnp.int32(0), jnp.int32(0)
    entries = []
    for s in offsets:
        right_w = jnp.where(s >= 0, jnp.minimum(s + 2, cols), jnp.where(s == -1, 1, 0))
        left_w = jnp.where(s < 0, jnp.minimum(1 - s, cols), jnp.where(s == 0, 1, 0))
        entries.append((s, right_at, right_w, left_at, left_w))
        right_at = right_at + right_w
        left_at = left_at + left_w
    return entries, right_at, left_at


def read_offsets(words_ref, rows, cols):
    words = [words_ref[0, k] for k in range((rows + 3) // 4)]
    return [
        jnp.bitwise_and(lax.shift_right_logical(words[i // 4], 8 * (i % 4)), 2 * cols - 1) - cols
        for i in range(rows)
    ]


def any_of(flags):
    result = flags[0]
    for flag in flags[1:]:
        result = result | flag
    return result


def pack_kernel(
    tile_hbm, col_hbm, x_hbm, fx_hbm, fy_hbm,
    units_ref, far_right_ref, far_left_ref, tail_ref, words_ref, index_ref,
    tile_ref, col_ref, x_ref, fx_ref, fy_ref, small_sems, row_sems,
):
    rows, levels, cols = x_ref.shape
    half = units_ref.shape[1]
    unit = cols // 2
    most = 2 * rows
    room = units_ref.shape[0] // 2
    small = [
        pltpu.make_async_copy(src, dst, small_sems.at[k])
        for k, (src, dst) in enumerate(
            [(tile_hbm, tile_ref), (col_hbm, col_ref), (fx_hbm, fx_ref), (fy_hbm, fy_ref)]
        )
    ]
    for copy in small:
        copy.start()
    big = [pltpu.make_async_copy(x_hbm.at[i], x_ref.at[i], row_sems.at[i]) for i in range(rows)]
    for copy in big:
        copy.start()
    for copy in small:
        copy.wait()
    offsets = [tile_ref[i] * cols + col_ref[i] for i in range(rows)]
    entries, right_total, left_total = plan(offsets, cols)
    r = (right_total + unit - 1) // unit
    l = (left_total + unit - 1) // unit
    first = jnp.where(r == 0, 0, most + 1 + (r - 1) * (most + 2) - (r - 1) * r // 2)
    index_ref[0] = first + l

    lane = lax.broadcasted_iota(jnp.int32, (PIECE, cols), 1)
    low_lane = jnp.bitwise_and(lane, unit - 1)
    low_half = lane < unit
    sub = lax.broadcasted_iota(jnp.int32, (PIECE, cols), 0)
    words = jnp.zeros((PIECE, cols), jnp.int32)
    for k in range((rows + 3) // 4):
        word = jnp.int32(0)
        for i in range(4 * k, min(4 * k + 4, rows)):
            word = word | lax.shift_left(offsets[i] + cols, 8 * (i % 4))
        words = jnp.where(lane == k, word, words)
    words_ref[...] = words
    for i in range(rows):
        tail_ref[i] = jnp.where(sub == 0, fx_ref[i : i + 1, :], fy_ref[i : i + 1, :])

    def place(i, base, start, at, width):
        shift = jnp.bitwise_and(at - start, cols - 1)
        window = at // cols
        masks = []
        for k in range(4):
            place_of = (2 * window + k) * unit + low_lane
            masks.append((place_of >= at) & (place_of < at + width))
        for level in range(0, half, PIECE):
            lo = x_ref[i, level : level + PIECE, :]
            hi = x_ref[i, half + level : half + level + PIECE, :] if half + level < levels else tail_ref[i]
            lo = pltpu.roll(lo, shift, 1)
            hi = pltpu.roll(hi, shift, 1)
            even = jnp.where(low_half, lo, pltpu.roll(hi, unit, 1))
            odd = jnp.where(low_half, pltpu.roll(lo, unit, 1), hi)
            for k in range(4):
                u = base + 2 * window + k
                old = units_ref[u, level : level + PIECE, :]
                units_ref[u, level : level + PIECE, :] = jnp.where(masks[k], odd if k % 2 else even, old)

    for i in range(rows):
        s, right_at, right_w, left_at, left_w = entries[i]
        goes_right = s >= 0
        big[i].wait()
        place(
            i,
            jnp.where(goes_right, 0, room),
            jnp.where(goes_right, cols - right_w, 0),
            jnp.where(goes_right, right_at, left_at),
            jnp.where(goes_right, right_w, left_w),
        )

    def place_far(i, far_ref, column):
        for k in range(2):
            block = far_ref[k * PIECE : (k + 1) * PIECE, :]
            for f in range(half // PIECE):
                level = (2 * f + k) * PIECE
                value = x_ref[i, level : level + PIECE, :] if level < levels else tail_ref[i]
                to = rows * f + i
                block = jnp.where(lane == to, pltpu.roll(value, (to - column) % cols, 1), block)
            far_ref[k * PIECE : (k + 1) * PIECE, :] = block

    @pl.when(any_of([(s == 0) | (s == -1) | (s == cols - 1) | (s == -cols) for s in offsets]))
    def _():
        for i in range(rows):
            s, right_at, right_w, left_at, left_w = entries[i]

            @pl.when((s == 0) | (s == -1))
            def _():
                zero = s == 0
                place(
                    i, jnp.where(zero, room, 0), jnp.where(zero, 0, cols - 1), jnp.where(zero, left_at, right_at), 1
                )

            @pl.when(s == cols - 1)
            def _():
                place_far(i, far_right_ref, cols - 1)

            @pl.when(s == -cols)
            def _():
                place_far(i, far_left_ref, 0)


def split(value):
    high = value.astype(jnp.bfloat16)
    return high, (value - high.astype(jnp.float32)).astype(jnp.bfloat16)


def dot_nt(left, right):
    return lax.dot_general(left, right, (((1,), (1,)), ((), ())), preferred_element_type=jnp.float32)


def spread_kernel(wanted, words_ref, x_ref, tail_ref, units_ref, far_right_ref, far_left_ref, *refs):
    out_refs, other_ref = refs[:-1], refs[-1]
    rows, levels, cols = x_ref.shape
    half = units_ref.shape[1]
    unit = cols // 2
    room = units_ref.shape[0] // 2
    offsets = read_offsets(words_ref, rows, cols)
    entries, _, _ = plan(offsets, cols)
    lane = lax.broadcasted_iota(jnp.int32, (1, cols), 1)
    low_lane = jnp.bitwise_and(lane, unit - 1)
    low_half = lane < unit
    to = lax.broadcasted_iota(jnp.int32, (cols, cols), 0)
    chosen = sorted({w[0] for w in wanted})
    seen = set()

    def matrices(fractions, column, which):
        b_of = to - column + 1
        wx = wx_weights(fractions[0:1, :])
        wy = wx_weights(fractions[1:2, :])
        along = jnp.where(b_of == 0, wx[0], 0.0)
        for b in range(1, 4):
            along = jnp.where(b_of == b, wx[b], along)
        return [split(along * wy[a]) for a in which]

    for i in chosen:
        mine = [w[1:] for w in wanted if w[0] == i]
        which = [a for a, _, _ in mine]
        s, right_at, right_w, left_at, left_w = entries[i]
        goes_right = s >= 0
        at = jnp.where(goes_right, right_at, left_at)
        width = jnp.where(goes_right, right_w, left_w)
        base = jnp.where(goes_right, 0, room) + 2 * (at // cols)
        om = jnp.bitwise_and(at, cols - 1)
        place = jnp.bitwise_and(lane - at, cols - 1)
        held = place < width
        start = jnp.where(goes_right, s - width, s + cols)

        piece = [units_ref[base + k] for k in range(4)]
        even = jnp.where(low_lane >= om, piece[0], piece[2])
        odd = jnp.where(low_lane + unit >= om, piece[1], piece[3])
        got = [
            jnp.where(held, jnp.where(low_half, even, pltpu.roll(odd, unit, 1)), 0.0),
            jnp.where(held, jnp.where(low_half, pltpu.roll(even, unit, 1), odd), 0.0),
        ]
        home = [
            x_ref[i, 0:half, :],
            jnp.concatenate([x_ref[i, half:levels, :], jnp.zeros((2 * half - levels, cols), jnp.float32)], axis=0),
        ]
        from_home = matrices(tail_ref[i], lane + s, which)
        from_got = matrices(got[1][half - PIECE : half, :], jnp.where(held, start + place, -2 * cols), which)
        ones = [
            jnp.concatenate([jnp.concatenate([h[part], g[part]], axis=1) for h, g in zip(from_home, from_got)], axis=0)
            for part in range(2)
        ]
        for p in range(2):
            home_parts, got_parts = split(home[p]), split(got[p])
            high, low = [jnp.concatenate([home_parts[part], got_parts[part]], axis=1) for part in range(2)]
            total = dot_nt(high, ones[0]) + (dot_nt(high, ones[1]) + dot_nt(low, ones[0]))
            size = half if p == 0 else levels - half
            for n, (a, out, k) in enumerate(mine):
                value = total[0:size, n * cols : (n + 1) * cols]
                if (out, k) in seen:
                    value = value + out_refs[out][k, p * half : p * half + size, :]
                out_refs[out][k, p * half : p * half + size, :] = value
        seen.update((out, k) for _, out, k in mine)

    def add_other(i, lane_to, b):
        fractions = other_ref[2 * half - PIECE : 2 * half, :]
        wx = wx_weights(fractions[0:1, :])[b]
        wy = wx_weights(fractions[1:2, :])
        for row, a, out, k in wanted:
            if row == i:
                weight = wx * wy[a]
                for level in range(0, levels, PIECE):
                    old = out_refs[out][k, level : level + PIECE, :]
                    new = old + other_ref[level : level + PIECE, :] * weight
                    out_refs[out][k, level : level + PIECE, :] = jnp.where(lane == lane_to, new, old)

    def fetch_unit(u, place, lane_to):
        for level in range(0, half, PIECE):
            value = units_ref[u, level : level + PIECE, :]
            other_ref[level : level + PIECE, :] = pltpu.roll(value, jnp.bitwise_and(lane_to - place, cols - 1), 1)
            other_ref[half + level : half + level + PIECE, :] = pltpu.roll(
                value, jnp.bitwise_and(lane_to - place - unit, cols - 1), 1
            )

    def fetch_far(i, far_ref, lane_to):
        for k in range(2):
            block = far_ref[k * PIECE : (k + 1) * PIECE, :]
            for f in range(half // PIECE):
                level = (2 * f + k) * PIECE
                other_ref[level : level + PIECE, :] = pltpu.roll(block, (lane_to - rows * f - i) % cols, 1)

    @pl.when(any_of([(s == 0) | (s == -1) | (s == cols - 1) | (s == -cols) for s in (offsets[i] for i in chosen)]))
    def _():
        for i in chosen:
            s, right_at, right_w, left_at, left_w = entries[i]

            @pl.when(s == 0)
            def _():
                fetch_unit(room + left_at // unit, jnp.bitwise_and(left_at, unit - 1), cols - 1)
                add_other(i, cols - 1, 0)

            @pl.when(s == -1)
            def _():
                fetch_unit(right_at // unit, jnp.bitwise_and(right_at, unit - 1), 0)
                add_other(i, 0, 3)

            @pl.when(s == cols - 1)
            def _():
                fetch_far(i, far_right_ref, 0)
                add_other(i, 0, 3)

            @pl.when(s == -cols)
            def _():
                fetch_far(i, far_left_ref, cols - 1)
                add_other(i, cols - 1, 0)


def vertical_kernel(mid_ref, from_prev_ref, from_next_ref, inverse_ref, coupling_hbm, out_ref, matrix_ref, coupling_ref, sem):
    rows, tracers, levels, cols = out_ref.shape
    size = inverse_ref.shape[2]
    level_of = lax.broadcasted_iota(jnp.int32, (levels, cols), 0)
    dot = functools.partial(jnp.dot, preferred_element_type=jnp.float32)
    copy = pltpu.make_async_copy(coupling_hbm, coupling_ref, sem)
    copy.start()
    matrix_ref[...] = jnp.zeros(matrix_ref.shape, jnp.float32)
    copy.wait()
    for i in range(rows):
        matrix_ref[0:size, 0:size] = inverse_ref[i, 0]
        matrix_ref[size:levels, size:levels] = inverse_ref[i, 1]
        matrix = matrix_ref[...]
        m_hi = matrix.astype(jnp.bfloat16)
        m_lo = (matrix - m_hi.astype(jnp.float32)).astype(jnp.bfloat16)
        edge = jnp.where(
            level_of[:, 0:1] < size, matrix[:, size - 1 : size], matrix[:, size : size + 1]
        )
        edge = jnp.broadcast_to(edge, (levels, cols))
        for t in range(tracers):
            field = mid_ref[i, t]
            if i < 2:
                field = field + from_prev_ref[i, t]
            if i == rows - 1:
                field = field + from_next_ref[0, t]
            f_hi = field.astype(jnp.bfloat16)
            f_lo = (field - f_hi.astype(jnp.float32)).astype(jnp.bfloat16)
            first = dot(m_hi, f_hi) + (dot(m_hi, f_lo) + dot(m_lo, f_hi))
            coupling = coupling_ref[i : i + 1, :]
            other = jnp.where(
                level_of < size, coupling * first[size : size + 1, :], coupling * first[size - 1 : size, :]
            )
            out_ref[i, t] = first + edge * other


def on_device(adjoint_in, frac_x, frac_y, dep_tile, dep_col, block_inverse, coupling):
    rows, tracers, levels, cols = adjoint_in.shape
    flat = tracers * levels
    half = (flat + 2 + 2 * PIECE - 1) // (2 * PIECE) * PIECE
    most = 2 * rows
    room = most + 4
    x = adjoint_in.reshape(rows, flat, cols)
    f32 = jnp.float32
    vmem = pl.BlockSpec(memory_space=pltpu.VMEM)
    smem = pl.BlockSpec(memory_space=pltpu.SMEM)
    params = pltpu.CompilerParams(vmem_limit_bytes=VMEM_BYTES)

    units, far_right, far_left, tail, words, index = pl.pallas_call(
        pack_kernel,
        name="pack",
        out_shape=(
            jax.ShapeDtypeStruct((2 * room, half, cols), f32),
            jax.ShapeDtypeStruct((2 * PIECE, cols), f32),
            jax.ShapeDtypeStruct((2 * PIECE, cols), f32),
            jax.ShapeDtypeStruct((rows, PIECE, cols), f32),
            jax.ShapeDtypeStruct((PIECE, cols), jnp.int32),
            jax.ShapeDtypeStruct((1,), jnp.int32),
        ),
        in_specs=[pl.BlockSpec(memory_space=pltpu.HBM)] * 5,
        out_specs=(vmem, vmem, vmem, vmem, vmem, smem),
        scratch_shapes=[
            pltpu.SMEM((rows,), jnp.int32),
            pltpu.SMEM((rows,), jnp.int32),
            pltpu.VMEM((rows, flat, cols), f32),
            pltpu.VMEM((rows, cols), f32),
            pltpu.VMEM((rows, cols), f32),
            pltpu.SemaphoreType.DMA((4,)),
            pltpu.SemaphoreType.DMA((rows,)),
        ],
        compiler_params=pltpu.CompilerParams(vmem_limit_bytes=PACK_BYTES),
    )(dep_tile, dep_col, x, frac_x, frac_y)

    def exchange(right_units, left_units):
        def run(units, *far):
            sends, places = [], []
            if right_units:
                sends.append((units[:right_units], 1))
                places.append((0, 0, 0))
            if left_units:
                sends.append((units[room : room + left_units], -1))
                places.append((room, 0, 0))
            sends.append((far[0], 2))
            sends.append((far[1], -2))
            taken = lax.optimization_barrier(tuple(value for value, _ in sends))
            arrived = [passed_along(value, "lon", by) for value, (_, by) in zip(taken, sends)]
            arrived = lax.optimization_barrier(tuple(arrived))
            for place, value in zip(places, arrived):
                units = lax.dynamic_update_slice(units, value, place)
            return units, arrived[-2], arrived[-1]

        return run

    branches = [
        exchange(r, l) for r in range(most + 1) for l in range(most + 1) if r + l <= most + 1
    ]
    units, far_right, far_left = lax.switch(index[0], branches, units, far_right, far_left)

    def spread(name, wanted, sizes):
        return pl.pallas_call(
            functools.partial(spread_kernel, wanted),
            name=name,
            out_shape=tuple(jax.ShapeDtypeStruct((n, flat, cols), f32) for n in sizes),
            in_specs=[vmem] * 6,
            out_specs=(vmem,) * len(sizes),
            scratch_shapes=[pltpu.VMEM((2 * half, cols), f32)],
            compiler_params=params,
        )(words, x, tail, units, far_right, far_left)

    rim, middle = [], []
    for i in range(rows):
        for a in range(4):
            t = i + a - 1
            if t < 0:
                rim.append((i, a, 0, 0))
            elif t >= rows:
                rim.append((i, a, 1, t - rows))
            else:
                middle.append((i, a, 0, t))
    down, up = spread("rim", rim, (1, 2))
    from_prev = shifted(up, "lat", 1)
    from_next = shifted(down, "lat", -1)
    (mid,) = spread("middle", middle, (rows,))

    return pl.pallas_call(
        vertical_kernel,
        name="vertical",
        out_shape=jax.ShapeDtypeStruct(adjoint_in.shape, f32),
        in_specs=[vmem, vmem, vmem, vmem, pl.BlockSpec(memory_space=pltpu.HBM)],
        out_specs=vmem,
        scratch_shapes=[
            pltpu.VMEM((levels, levels), f32),
            pltpu.VMEM((rows, cols), f32),
            pltpu.SemaphoreType.DMA(()),
        ],
        compiler_params=params,
    )(
        mid.reshape(rows, tracers, levels, cols),
        from_prev.reshape(2, tracers, levels, cols),
        from_next.reshape(1, tracers, levels, cols),
        block_inverse,
        coupling,
    )


def solution(mesh):
    return jax.shard_map(
        on_device,
        mesh=mesh,
        in_specs=(
            P("lat", None, None, "lon"),
            P("lat", "lon"),
            P("lat", "lon"),
            P("lat"),
            P("lat"),
            P("lat", None, None, None),
            P("lat", "lon"),
        ),
        out_specs=P("lat", None, None, "lon"),
        check_vma=False,
    )
```

```python
import functools

import jax
import jax.numpy as jnp
from jax import lax
from jax.experimental import pallas as pl
from jax.experimental.pallas import tpu as pltpu
from jax.sharding import PartitionSpec as P

PIECE = 8
VMEM_BYTES = 48 * 1024 * 1024
PACK_BYTES = 61 * 1024 * 1024


def passed_along(x, axis, by):
    devices = lax.axis_size(axis)
    return lax.ppermute(x, axis, [(i, (i + by) % devices) for i in range(devices)])


def swapped(x, axis, first):
    devices = lax.axis_size(axis)
    pairs = [(i, i + 1) for i in range(first, devices - 1, 2)]
    return lax.ppermute(x, axis, pairs + [(j, i) for i, j in pairs])


def wx_weights(f):
    return [
        -f * (f - 1.0) * (f - 2.0) / 6.0,
        (f + 1.0) * (f - 1.0) * (f - 2.0) / 2.0,
        -(f + 1.0) * f * (f - 2.0) / 2.0,
        (f + 1.0) * f * (f - 1.0) / 6.0,
    ]


def plan(offsets, cols):
    right_at, left_at = jnp.int32(0), jnp.int32(0)
    entries = []
    for s in offsets:
        right_w = jnp.where(s >= 0, jnp.minimum(s + 2, cols), jnp.where(s == -1, 1, 0))
        left_w = jnp.where(s < 0, jnp.minimum(1 - s, cols), jnp.where(s == 0, 1, 0))
        entries.append((s, right_at, right_w, left_at, left_w))
        right_at = right_at + right_w
        left_at = left_at + left_w
    return entries, right_at, left_at


def read_offsets(words_ref, rows, cols):
    words = [words_ref[0, k] for k in range((rows + 3) // 4)]
    return [
        jnp.bitwise_and(lax.shift_right_logical(words[i // 4], 8 * (i % 4)), 2 * cols - 1) - cols
        for i in range(rows)
    ]


def any_of(flags):
    result = flags[0]
    for flag in flags[1:]:
        result = result | flag
    return result


def pack_kernel(
    tile_hbm, col_hbm, x_hbm, fx_hbm, fy_hbm, coupling_hbm,
    units_ref, far_ref, tail_ref, words_ref, index_ref,
    tile_ref, col_ref, x_ref, fx_ref, fy_ref, coupling_ref, small_sems, row_sems,
):
    rows, levels, cols = x_ref.shape
    half = units_ref.shape[1]
    unit = cols // 2
    most = 2 * rows
    room = units_ref.shape[0] // 2
    small = [
        pltpu.make_async_copy(src, dst, small_sems.at[k])
        for k, (src, dst) in enumerate(
            [
                (tile_hbm, tile_ref),
                (col_hbm, col_ref),
                (fx_hbm, fx_ref),
                (fy_hbm, fy_ref),
                (coupling_hbm, coupling_ref),
            ]
        )
    ]
    for copy in small:
        copy.start()
    big = [pltpu.make_async_copy(x_hbm.at[i], x_ref.at[i], row_sems.at[i]) for i in range(rows)]
    for copy in big:
        copy.start()
    for copy in small:
        copy.wait()
    offsets = [tile_ref[i] * cols + col_ref[i] for i in range(rows)]
    entries, right_total, left_total = plan(offsets, cols)
    r = (right_total + unit - 1) // unit
    l = (left_total + unit - 1) // unit
    first = jnp.where(r == 0, 0, most + 1 + (r - 1) * (most + 2) - (r - 1) * r // 2)
    index_ref[0] = first + l

    lane = lax.broadcasted_iota(jnp.int32, (PIECE, cols), 1)
    low_lane = jnp.bitwise_and(lane, unit - 1)
    low_half = lane < unit
    sub = lax.broadcasted_iota(jnp.int32, (PIECE, cols), 0)
    words = jnp.zeros((PIECE, cols), jnp.int32)
    for k in range((rows + 3) // 4):
        word = jnp.int32(0)
        for i in range(4 * k, min(4 * k + 4, rows)):
            word = word | lax.shift_left(offsets[i] + cols, 8 * (i % 4))
        words = jnp.where(lane == k, word, words)
    odd_band = jnp.bitwise_and(lax.axis_index("lat"), 1)
    words_ref[...] = jnp.where(lane == cols - 1, odd_band, words)
    for i in range(rows):
        tail_ref[i] = jnp.where(
            sub == 0, fx_ref[i : i + 1, :], jnp.where(sub == 1, fy_ref[i : i + 1, :], coupling_ref[i : i + 1, :])
        )

    def place(i, base, start, at, width):
        shift = jnp.bitwise_and(at - start, cols - 1)
        window = at // cols
        masks = []
        for k in range(4):
            place_of = (2 * window + k) * unit + low_lane
            masks.append((place_of >= at) & (place_of < at + width))
        for level in range(0, half, PIECE):
            lo = x_ref[i, level : level + PIECE, :]
            hi = x_ref[i, half + level : half + level + PIECE, :] if half + level < levels else tail_ref[i]
            lo = pltpu.roll(lo, shift, 1)
            hi = pltpu.roll(hi, shift, 1)
            even = jnp.where(low_half, lo, pltpu.roll(hi, unit, 1))
            odd = jnp.where(low_half, pltpu.roll(lo, unit, 1), hi)
            for k in range(4):
                u = base + 2 * window + k
                old = units_ref[u, level : level + PIECE, :]
                units_ref[u, level : level + PIECE, :] = jnp.where(masks[k], odd if k % 2 else even, old)

    for i in range(rows):
        s, right_at, right_w, left_at, left_w = entries[i]
        goes_right = s >= 0
        big[i].wait()
        place(
            i,
            jnp.where(goes_right, 0, room),
            jnp.where(goes_right, cols - right_w, 0),
            jnp.where(goes_right, right_at, left_at),
            jnp.where(goes_right, right_w, left_w),
        )

    def place_far(i, which, column):
        for k in range(2):
            block = far_ref[which, k * PIECE : (k + 1) * PIECE, :]
            for f in range(half // PIECE):
                level = (2 * f + k) * PIECE
                value = x_ref[i, level : level + PIECE, :] if level < levels else tail_ref[i]
                to = rows * f + i
                block = jnp.where(lane == to, pltpu.roll(value, (to - column) % cols, 1), block)
            far_ref[which, k * PIECE : (k + 1) * PIECE, :] = block

    @pl.when(any_of([(s == 0) | (s == -1) | (s == cols - 1) | (s == -cols) for s in offsets]))
    def _():
        for i in range(rows):
            s, right_at, right_w, left_at, left_w = entries[i]

            @pl.when((s == 0) | (s == -1))
            def _():
                zero = s == 0
                place(
                    i, jnp.where(zero, room, 0), jnp.where(zero, 0, cols - 1), jnp.where(zero, left_at, right_at), 1
                )

            @pl.when(s == cols - 1)
            def _():
                place_far(i, 0, cols - 1)

            @pl.when(s == -cols)
            def _():
                place_far(i, 1, 0)


def split(value):
    high = value.astype(jnp.bfloat16)
    return high, (value - high.astype(jnp.float32)).astype(jnp.bfloat16)


def dot_nt(left, right):
    return lax.dot_general(left, right, (((1,), (1,)), ((), ())), preferred_element_type=jnp.float32)


def spread(wanted, out_places, out_ref, words_ref, x_ref, tail_ref, units_ref, far_ref, other_ref):
    rows, levels, cols = x_ref.shape
    half = units_ref.shape[1]
    unit = cols // 2
    room = units_ref.shape[0] // 2
    offsets = read_offsets(words_ref, rows, cols)
    entries, _, _ = plan(offsets, cols)
    lane = lax.broadcasted_iota(jnp.int32, (1, cols), 1)
    low_lane = jnp.bitwise_and(lane, unit - 1)
    low_half = lane < unit
    to = lax.broadcasted_iota(jnp.int32, (cols, cols), 0)
    chosen = sorted({w[0] for w in wanted})
    seen = set()
    at_of = out_places(words_ref[0, cols - 1]) if out_places else {w[2]: w[2] for w in wanted}

    def matrices(fractions, column, which):
        b_of = to - column + 1
        wx = wx_weights(fractions[0:1, :])
        wy = wx_weights(fractions[1:2, :])
        along = jnp.where(b_of == 0, wx[0], 0.0)
        for b in range(1, 4):
            along = jnp.where(b_of == b, wx[b], along)
        return [split(along * wy[a]) for a in which]

    for i in chosen:
        mine = [w[1:] for w in wanted if w[0] == i]
        which = [a for a, _ in mine]
        s, right_at, right_w, left_at, left_w = entries[i]
        goes_right = s >= 0
        at = jnp.where(goes_right, right_at, left_at)
        width = jnp.where(goes_right, right_w, left_w)
        base = jnp.where(goes_right, 0, room) + 2 * (at // cols)
        om = jnp.bitwise_and(at, cols - 1)
        place = jnp.bitwise_and(lane - at, cols - 1)
        held = place < width
        start = jnp.where(goes_right, s - width, s + cols)

        piece = [units_ref[base + k] for k in range(4)]
        even = jnp.where(low_lane >= om, piece[0], piece[2])
        odd = jnp.where(low_lane + unit >= om, piece[1], piece[3])
        got = [
            jnp.where(held, jnp.where(low_half, even, pltpu.roll(odd, unit, 1)), 0.0),
            jnp.where(held, jnp.where(low_half, pltpu.roll(even, unit, 1), odd), 0.0),
        ]
        home = [
            x_ref[i, 0:half, :],
            jnp.concatenate([x_ref[i, half:levels, :], jnp.zeros((2 * half - levels, cols), jnp.float32)], axis=0),
        ]
        from_home = matrices(tail_ref[i], lane + s, which)
        from_got = matrices(got[1][half - PIECE : half, :], jnp.where(held, start + place, -2 * cols), which)
        ones = [
            jnp.concatenate([jnp.concatenate([h[part], g[part]], axis=1) for h, g in zip(from_home, from_got)], axis=0)
            for part in range(2)
        ]
        for p in range(2):
            home_parts, got_parts = split(home[p]), split(got[p])
            high, low = [jnp.concatenate([home_parts[part], got_parts[part]], axis=1) for part in range(2)]
            total = dot_nt(high, ones[0]) + (dot_nt(high, ones[1]) + dot_nt(low, ones[0]))
            size = half if p == 0 else levels - half
            for n, (a, k) in enumerate(mine):
                value = total[0:size, n * cols : (n + 1) * cols]
                if k in seen:
                    value = value + out_ref[at_of[k], p * half : p * half + size, :]
                out_ref[at_of[k], p * half : p * half + size, :] = value
        seen.update(k for _, k in mine)

    def add_other(i, lane_to, b):
        fractions = other_ref[2 * half - PIECE : 2 * half, :]
        wx = wx_weights(fractions[0:1, :])[b]
        wy = wx_weights(fractions[1:2, :])
        for row, a, k in wanted:
            if row == i:
                weight = wx * wy[a]
                for level in range(0, levels, PIECE):
                    old = out_ref[at_of[k], level : level + PIECE, :]
                    new = old + other_ref[level : level + PIECE, :] * weight
                    out_ref[at_of[k], level : level + PIECE, :] = jnp.where(lane == lane_to, new, old)

    def fetch_unit(u, place, lane_to):
        for level in range(0, half, PIECE):
            value = units_ref[u, level : level + PIECE, :]
            other_ref[level : level + PIECE, :] = pltpu.roll(value, jnp.bitwise_and(lane_to - place, cols - 1), 1)
            other_ref[half + level : half + level + PIECE, :] = pltpu.roll(
                value, jnp.bitwise_and(lane_to - place - unit, cols - 1), 1
            )

    def fetch_far(i, which, lane_to):
        for k in range(2):
            block = far_ref[which, k * PIECE : (k + 1) * PIECE, :]
            for f in range(half // PIECE):
                level = (2 * f + k) * PIECE
                other_ref[level : level + PIECE, :] = pltpu.roll(block, (lane_to - rows * f - i) % cols, 1)

    @pl.when(any_of([(s == 0) | (s == -1) | (s == cols - 1) | (s == -cols) for s in (offsets[i] for i in chosen)]))
    def _():
        for i in chosen:
            s, right_at, right_w, left_at, left_w = entries[i]

            @pl.when(s == 0)
            def _():
                fetch_unit(room + left_at // unit, jnp.bitwise_and(left_at, unit - 1), cols - 1)
                add_other(i, cols - 1, 0)

            @pl.when(s == -1)
            def _():
                fetch_unit(right_at // unit, jnp.bitwise_and(right_at, unit - 1), 0)
                add_other(i, 0, 3)

            @pl.when(s == cols - 1)
            def _():
                fetch_far(i, 0, 0)
                add_other(i, 0, 3)

            @pl.when(s == -cols)
            def _():
                fetch_far(i, 1, cols - 1)
                add_other(i, cols - 1, 0)


def rim_kernel(
    wanted, words_ref, x_ref, tail_ref, units_ref, far_ref, out_ref, other_ref
):
    def out_places(odd_band):
        up, down = jnp.where(odd_band == 1, 0, 2), jnp.where(odd_band == 1, 2, 0)
        return {-1: down, 0: up, 1: up + 1}

    spread(
        wanted, out_places, out_ref, words_ref, x_ref, tail_ref, units_ref, far_ref, other_ref
    )


def products(parts, field):
    high, low = split(field)
    dot = functools.partial(jnp.dot, preferred_element_type=jnp.float32)
    return dot(parts[0], high) + (dot(parts[0], low) + dot(parts[1], high))


def middle_kernel(
    wanted, words_ref, x_ref, tail_ref, units_ref, far_ref, inverse_ref,
    first_ref, parts_ref, edge_ref,
    mid_ref, matrix_ref, other_ref,
):
    rows, tracers, levels, cols = first_ref.shape
    size = inverse_ref.shape[2]
    spread(wanted, None, mid_ref, words_ref, x_ref, tail_ref, units_ref, far_ref, other_ref)
    matrix_ref[...] = jnp.zeros(matrix_ref.shape, jnp.float32)
    level_of = lax.broadcasted_iota(jnp.int32, (levels, 1), 0)
    for i in range(rows):
        matrix_ref[0:size, 0:size] = inverse_ref[i, 0]
        matrix_ref[size:levels, size:levels] = inverse_ref[i, 1]
        matrix = matrix_ref[...]
        parts = split(matrix)
        parts_ref[i, 0] = parts[0]
        parts_ref[i, 1] = parts[1]
        edge = jnp.where(level_of < size, matrix[0:levels, size - 1 : size], matrix[0:levels, size : size + 1])
        edge_ref[i] = jnp.broadcast_to(edge, (levels, cols))
        for t in range(tracers):
            first_ref[i, t] = products(parts, mid_ref[i, t * levels : (t + 1) * levels, :])[0:levels]


def finish_kernel(words_ref, tail_ref, first_ref, parts_ref, edge_ref, cross_ref, chip_ref, out_hbm, out_ref, sems):
    rows, tracers, levels, cols = first_ref.shape
    size = levels // 2
    odd_band = words_ref[0, cols - 1] == 1
    level_of = lax.broadcasted_iota(jnp.int32, (levels, cols), 0)
    copies = []
    for i in sorted(range(rows), key=lambda i: i < 2 or i == rows - 1):
        parts = [parts_ref[i, 0], parts_ref[i, 1]]
        coupling = tail_ref[i, 2:3, :]
        for t in range(tracers):
            first = first_ref[i, t]
            if i < 2:
                rim = jnp.where(odd_band, chip_ref[i, t], cross_ref[i, t])
                first = first + products(parts, rim)[0:levels]
            if i == rows - 1:
                rim = jnp.where(odd_band, cross_ref[0, t], chip_ref[0, t])
                first = first + products(parts, rim)[0:levels]
            other = jnp.where(
                level_of < size, coupling * first[size : size + 1, :], coupling * first[size - 1 : size, :]
            )
            out_ref[i, t] = first + edge_ref[i] * other
        copies.append(pltpu.make_async_copy(out_ref.at[i], out_hbm.at[i], sems.at[i]))
        copies[-1].start()
    for copy in copies:
        copy.wait()


def on_device(adjoint_in, frac_x, frac_y, dep_tile, dep_col, block_inverse, coupling):
    rows, tracers, levels, cols = adjoint_in.shape
    flat = tracers * levels
    half = (flat + 2 + 2 * PIECE - 1) // (2 * PIECE) * PIECE
    most = 2 * rows
    room = most + 4
    x = adjoint_in.reshape(rows, flat, cols)
    f32 = jnp.float32
    vmem = pl.BlockSpec(memory_space=pltpu.VMEM)
    smem = pl.BlockSpec(memory_space=pltpu.SMEM)
    params = pltpu.CompilerParams(vmem_limit_bytes=VMEM_BYTES)

    units, far, tail, words, index = pl.pallas_call(
        pack_kernel,
        name="pack",
        out_shape=(
            jax.ShapeDtypeStruct((2 * room, half, cols), f32),
            jax.ShapeDtypeStruct((2, 2 * PIECE, cols), f32),
            jax.ShapeDtypeStruct((rows, PIECE, cols), f32),
            jax.ShapeDtypeStruct((PIECE, cols), jnp.int32),
            jax.ShapeDtypeStruct((1,), jnp.int32),
        ),
        in_specs=[pl.BlockSpec(memory_space=pltpu.HBM)] * 6,
        out_specs=(vmem, vmem, vmem, vmem, smem),
        scratch_shapes=[
            pltpu.SMEM((rows,), jnp.int32),
            pltpu.SMEM((rows,), jnp.int32),
            pltpu.VMEM((rows, flat, cols), f32),
            pltpu.VMEM((rows, cols), f32),
            pltpu.VMEM((rows, cols), f32),
            pltpu.VMEM((rows, cols), f32),
            pltpu.SemaphoreType.DMA((5,)),
            pltpu.SemaphoreType.DMA((rows,)),
        ],
        compiler_params=pltpu.CompilerParams(vmem_limit_bytes=PACK_BYTES),
    )(dep_tile, dep_col, x, frac_x, frac_y, coupling)

    def exchange(right_units, left_units):
        def run(units, far):
            sends, places = [], []
            if right_units:
                sends.append((units[:right_units], 1))
                places.append((0, 0, 0))
            if left_units:
                sends.append((units[room : room + left_units], -1))
                places.append((room, 0, 0))
            sends.append((far[0], 2))
            sends.append((far[1], -2))
            taken = lax.optimization_barrier(tuple(value for value, _ in sends))
            arrived = [passed_along(value, "lon", by) for value, (_, by) in zip(taken, sends)]
            arrived = lax.optimization_barrier(tuple(arrived))
            for place, value in zip(places, arrived):
                units = lax.dynamic_update_slice(units, value, place)
            far = lax.dynamic_update_slice(far, arrived[-2][None], (0, 0, 0))
            far = lax.dynamic_update_slice(far, arrived[-1][None], (1, 0, 0))
            return lax.optimization_barrier((units, far))

        return run

    branches = [
        exchange(r, l) for r in range(most + 1) for l in range(most + 1) if r + l <= most + 1
    ]
    units, far = lax.switch(index[0], branches, units, far)

    rim, middle = [], []
    for i in range(rows):
        for a in range(4):
            t = i + a - 1
            if t < 0:
                rim.append((i, a, t))
            elif t >= rows:
                rim.append((i, a, t - rows))
            else:
                middle.append((i, a, t))
    others = [pltpu.VMEM((2 * half, cols), f32)]
    operands = (words, x, tail, units, far)
    out = pl.pallas_call(
        functools.partial(rim_kernel, rim),
        name="rim",
        out_shape=jax.ShapeDtypeStruct((4, flat, cols), f32),
        in_specs=[vmem] * 5,
        out_specs=vmem,
        scratch_shapes=others,
        compiler_params=params,
    )(*operands)
    cross = swapped(out[:2], "lat", 1)
    chip = swapped(out[2:], "lat", 0)
    tall = (levels + 15) // 16 * 16
    first, parts, edge = pl.pallas_call(
        functools.partial(middle_kernel, middle),
        name="middle",
        out_shape=(
            jax.ShapeDtypeStruct(adjoint_in.shape, f32),
            jax.ShapeDtypeStruct((rows, 2, tall, levels), jnp.bfloat16),
            jax.ShapeDtypeStruct((rows, levels, cols), f32),
        ),
        in_specs=[vmem] * 6,
        out_specs=(vmem,) * 3,
        scratch_shapes=[pltpu.VMEM((rows, flat, cols), f32), pltpu.VMEM((tall, levels), f32)] + others,
        compiler_params=params,
    )(*operands, block_inverse)
    return pl.pallas_call(
        finish_kernel,
        name="finish",
        out_shape=jax.ShapeDtypeStruct(adjoint_in.shape, f32),
        in_specs=[vmem] * 7,
        out_specs=pl.BlockSpec(memory_space=pltpu.HBM),
        scratch_shapes=[pltpu.VMEM(adjoint_in.shape, f32), pltpu.SemaphoreType.DMA((rows,))],
        compiler_params=params,
    )(
        words, tail, first, parts, edge,
        cross.reshape(2, tracers, levels, cols), chip.reshape(2, tracers, levels, cols),
    )


def solution(mesh):
    return jax.shard_map(
        on_device,
        mesh=mesh,
        in_specs=(
            P("lat", None, None, "lon"),
            P("lat", "lon"),
            P("lat", "lon"),
            P("lat"),
            P("lat"),
            P("lat", None, None, None),
            P("lat", "lon"),
        ),
        out_specs=P("lat", None, None, "lon"),
        check_vma=False,
    )
```

```python
import functools

import jax
import jax.numpy as jnp
from jax import lax
from jax.experimental import pallas as pl
from jax.experimental.pallas import tpu as pltpu
from jax.sharding import PartitionSpec as P

PIECE = 8
LEAST = 3
VMEM_BYTES = 48 * 1024 * 1024
PACK_BYTES = 61 * 1024 * 1024


def passed_along(x, axis, by):
    devices = lax.axis_size(axis)
    return lax.ppermute(x, axis, [(i, (i + by) % devices) for i in range(devices)])


def swapped(x, axis, first):
    devices = lax.axis_size(axis)
    pairs = [(i, i + 1) for i in range(first, devices - 1, 2)]
    return lax.ppermute(x, axis, pairs + [(j, i) for i, j in pairs])


def wx_weights(f):
    return [
        -f * (f - 1.0) * (f - 2.0) / 6.0,
        (f + 1.0) * (f - 1.0) * (f - 2.0) / 2.0,
        -(f + 1.0) * f * (f - 2.0) / 2.0,
        (f + 1.0) * f * (f - 1.0) / 6.0,
    ]


def plan(offsets, cols):
    right_at, left_at = jnp.int32(0), jnp.int32(0)
    entries = []
    for s in offsets:
        right_w = jnp.where(s >= 0, jnp.minimum(s + 2, cols), jnp.where(s == -1, 1, 0))
        left_w = jnp.where(s < 0, jnp.minimum(1 - s, cols), jnp.where(s == 0, 1, 0))
        entries.append((s, right_at, right_w, left_at, left_w))
        right_at = right_at + right_w
        left_at = left_at + left_w
    return entries, right_at, left_at


def read_offsets(words_ref, rows, cols):
    words = [words_ref[0, k] for k in range((rows + 3) // 4)]
    return [
        jnp.bitwise_and(lax.shift_right_logical(words[i // 4], 8 * (i % 4)), 2 * cols - 1) - cols
        for i in range(rows)
    ]


def any_of(flags):
    result = flags[0]
    for flag in flags[1:]:
        result = result | flag
    return result


def pack_kernel(
    tile_hbm, col_hbm, x_hbm, fx_hbm, fy_hbm, coupling_hbm,
    units_ref, far_ref, tail_ref, words_ref, index_ref,
    tile_ref, col_ref, x_ref, fx_ref, fy_ref, coupling_ref, small_sems, row_sems,
):
    rows, levels, cols = x_ref.shape
    half = units_ref.shape[1]
    unit = cols // 2
    most = 2 * rows
    room = units_ref.shape[0] // 2
    small = [
        pltpu.make_async_copy(src, dst, small_sems.at[k])
        for k, (src, dst) in enumerate(
            [
                (tile_hbm, tile_ref),
                (col_hbm, col_ref),
                (fx_hbm, fx_ref),
                (fy_hbm, fy_ref),
                (coupling_hbm, coupling_ref),
            ]
        )
    ]
    for copy in small:
        copy.start()
    big = [pltpu.make_async_copy(x_hbm.at[i], x_ref.at[i], row_sems.at[i]) for i in range(rows)]
    for copy in big:
        copy.start()
    for copy in small:
        copy.wait()
    offsets = [tile_ref[i] * cols + col_ref[i] for i in range(rows)]
    entries, right_total, left_total = plan(offsets, cols)
    r = (right_total + unit - 1) // unit
    l = (left_total + unit - 1) // unit
    l = l + jnp.maximum(LEAST - r - l, 0)
    full = r + l == most
    r = jnp.where(full & (l == most), r + 1, r)
    l = jnp.where(full & (l < most), l + 1, l)
    both = r + l
    before = jnp.where(both > most, most * (most + 1) // 2 - 1, both * (both + 1) // 2)
    index_ref[0] = before - LEAST * (LEAST + 1) // 2 + r

    lane = lax.broadcasted_iota(jnp.int32, (PIECE, cols), 1)
    low_lane = jnp.bitwise_and(lane, unit - 1)
    low_half = lane < unit
    sub = lax.broadcasted_iota(jnp.int32, (PIECE, cols), 0)
    words = jnp.zeros((PIECE, cols), jnp.int32)
    for k in range((rows + 3) // 4):
        word = jnp.int32(0)
        for i in range(4 * k, min(4 * k + 4, rows)):
            word = word | lax.shift_left(offsets[i] + cols, 8 * (i % 4))
        words = jnp.where(lane == k, word, words)
    odd_band = jnp.bitwise_and(lax.axis_index("lat"), 1)
    words_ref[...] = jnp.where(sub == 1, odd_band, words)
    for i in range(rows):
        tail_ref[i] = jnp.where(
            sub == 0, fx_ref[i : i + 1, :], jnp.where(sub == 1, fy_ref[i : i + 1, :], coupling_ref[i : i + 1, :])
        )

    def place(i, base, start, at, width):
        shift = jnp.bitwise_and(at - start, cols - 1)
        window = at // cols
        masks = []
        for k in range(4):
            place_of = (2 * window + k) * unit + low_lane
            masks.append((place_of >= at) & (place_of < at + width))
        for level in range(0, half, PIECE):
            lo = x_ref[i, level : level + PIECE, :]
            hi = x_ref[i, half + level : half + level + PIECE, :] if half + level < levels else tail_ref[i]
            lo = pltpu.roll(lo, shift, 1)
            hi = pltpu.roll(hi, shift, 1)
            even = jnp.where(low_half, lo, pltpu.roll(hi, unit, 1))
            odd = jnp.where(low_half, pltpu.roll(lo, unit, 1), hi)
            for k in range(4):
                u = base + 2 * window + k
                old = units_ref[u, level : level + PIECE, :]
                units_ref[u, level : level + PIECE, :] = jnp.where(masks[k], odd if k % 2 else even, old)

    for i in range(rows):
        s, right_at, right_w, left_at, left_w = entries[i]
        goes_right = s >= 0
        big[i].wait()
        place(
            i,
            jnp.where(goes_right, 0, room),
            jnp.where(goes_right, cols - right_w, 0),
            jnp.where(goes_right, right_at, left_at),
            jnp.where(goes_right, right_w, left_w),
        )

    def place_far(i, which, column):
        for k in range(2):
            block = far_ref[which, k * PIECE : (k + 1) * PIECE, :]
            for f in range(half // PIECE):
                level = (2 * f + k) * PIECE
                value = x_ref[i, level : level + PIECE, :] if level < levels else tail_ref[i]
                to = rows * f + i
                block = jnp.where(lane == to, pltpu.roll(value, (to - column) % cols, 1), block)
            far_ref[which, k * PIECE : (k + 1) * PIECE, :] = block

    @pl.when(any_of([(s == 0) | (s == -1) | (s == cols - 1) | (s == -cols) for s in offsets]))
    def _():
        for i in range(rows):
            s, right_at, right_w, left_at, left_w = entries[i]

            @pl.when((s == 0) | (s == -1))
            def _():
                zero = s == 0
                place(
                    i, jnp.where(zero, room, 0), jnp.where(zero, 0, cols - 1), jnp.where(zero, left_at, right_at), 1
                )

            @pl.when(s == cols - 1)
            def _():
                place_far(i, 0, cols - 1)

            @pl.when(s == -cols)
            def _():
                place_far(i, 1, 0)


def split(value):
    high = value.astype(jnp.bfloat16)
    return high, (value - high.astype(jnp.float32)).astype(jnp.bfloat16)


def dot_nt(left, right):
    return lax.dot_general(left, right, (((1,), (1,)), ((), ())), preferred_element_type=jnp.float32)


def spread(wanted, out_places, out_ref, words_ref, x_ref, tail_ref, units_ref, far_ref, other_ref):
    rows, levels, cols = x_ref.shape
    half = units_ref.shape[1]
    unit = cols // 2
    room = units_ref.shape[0] // 2
    offsets = read_offsets(words_ref, rows, cols)
    entries, _, _ = plan(offsets, cols)
    lane = lax.broadcasted_iota(jnp.int32, (1, cols), 1)
    low_lane = jnp.bitwise_and(lane, unit - 1)
    low_half = lane < unit
    to = lax.broadcasted_iota(jnp.int32, (cols, cols), 0)
    chosen = sorted({w[0] for w in wanted})
    seen = set()
    at_of = out_places(words_ref[1, 0]) if out_places else {w[2]: w[2] for w in wanted}

    def matrices(fractions, column, which):
        b_of = to - column + 1
        wx = wx_weights(fractions[0:1, :])
        wy = wx_weights(fractions[1:2, :])
        along = jnp.where(b_of == 0, wx[0], 0.0)
        for b in range(1, 4):
            along = jnp.where(b_of == b, wx[b], along)
        return [split(along * wy[a]) for a in which]

    for i in chosen:
        mine = [w[1:] for w in wanted if w[0] == i]
        which = [a for a, _ in mine]
        s, right_at, right_w, left_at, left_w = entries[i]
        goes_right = s >= 0
        at = jnp.where(goes_right, right_at, left_at)
        width = jnp.where(goes_right, right_w, left_w)
        base = jnp.where(goes_right, 0, room) + 2 * (at // cols)
        om = jnp.bitwise_and(at, cols - 1)
        place = jnp.bitwise_and(lane - at, cols - 1)
        held = place < width
        start = jnp.where(goes_right, s - width, s + cols)

        piece = [units_ref[base + k] for k in range(4)]
        even = jnp.where(low_lane >= om, piece[0], piece[2])
        odd = jnp.where(low_lane + unit >= om, piece[1], piece[3])
        got = [
            jnp.where(held, jnp.where(low_half, even, pltpu.roll(odd, unit, 1)), 0.0),
            jnp.where(held, jnp.where(low_half, pltpu.roll(even, unit, 1), odd), 0.0),
        ]
        home = [
            x_ref[i, 0:half, :],
            jnp.concatenate([x_ref[i, half:levels, :], jnp.zeros((2 * half - levels, cols), jnp.float32)], axis=0),
        ]
        from_home = matrices(tail_ref[i], lane + s, which)
        from_got = matrices(got[1][half - PIECE : half, :], jnp.where(held, start + place, -2 * cols), which)
        ones = [
            jnp.concatenate([jnp.concatenate([h[part], g[part]], axis=1) for h, g in zip(from_home, from_got)], axis=0)
            for part in range(2)
        ]
        for p in range(2):
            home_parts, got_parts = split(home[p]), split(got[p])
            high, low = [jnp.concatenate([home_parts[part], got_parts[part]], axis=1) for part in range(2)]
            total = dot_nt(high, ones[0]) + (dot_nt(high, ones[1]) + dot_nt(low, ones[0]))
            size = half if p == 0 else levels - half
            for n, (a, k) in enumerate(mine):
                value = total[0:size, n * cols : (n + 1) * cols]
                if k in seen:
                    value = value + out_ref[at_of[k], p * half : p * half + size, :]
                out_ref[at_of[k], p * half : p * half + size, :] = value
        seen.update(k for _, k in mine)

    def add_other(i, lane_to, b):
        fractions = other_ref[2 * half - PIECE : 2 * half, :]
        wx = wx_weights(fractions[0:1, :])[b]
        wy = wx_weights(fractions[1:2, :])
        for row, a, k in wanted:
            if row == i:
                weight = wx * wy[a]
                for level in range(0, levels, PIECE):
                    old = out_ref[at_of[k], level : level + PIECE, :]
                    new = old + other_ref[level : level + PIECE, :] * weight
                    out_ref[at_of[k], level : level + PIECE, :] = jnp.where(lane == lane_to, new, old)

    def fetch_unit(u, place, lane_to):
        for level in range(0, half, PIECE):
            value = units_ref[u, level : level + PIECE, :]
            other_ref[level : level + PIECE, :] = pltpu.roll(value, jnp.bitwise_and(lane_to - place, cols - 1), 1)
            other_ref[half + level : half + level + PIECE, :] = pltpu.roll(
                value, jnp.bitwise_and(lane_to - place - unit, cols - 1), 1
            )

    def fetch_far(i, which, lane_to):
        for k in range(2):
            block = far_ref[which, k * PIECE : (k + 1) * PIECE, :]
            for f in range(half // PIECE):
                level = (2 * f + k) * PIECE
                other_ref[level : level + PIECE, :] = pltpu.roll(block, (lane_to - rows * f - i) % cols, 1)

    @pl.when(any_of([(s == 0) | (s == -1) | (s == cols - 1) | (s == -cols) for s in (offsets[i] for i in chosen)]))
    def _():
        for i in chosen:
            s, right_at, right_w, left_at, left_w = entries[i]

            @pl.when(s == 0)
            def _():
                fetch_unit(room + left_at // unit, jnp.bitwise_and(left_at, unit - 1), cols - 1)
                add_other(i, cols - 1, 0)

            @pl.when(s == -1)
            def _():
                fetch_unit(right_at // unit, jnp.bitwise_and(right_at, unit - 1), 0)
                add_other(i, 0, 3)

            @pl.when(s == cols - 1)
            def _():
                fetch_far(i, 0, 0)
                add_other(i, 0, 3)

            @pl.when(s == -cols)
            def _():
                fetch_far(i, 1, cols - 1)
                add_other(i, cols - 1, 0)


def rim_kernel(
    wanted, words_ref, x_ref, tail_ref, units_ref, far_ref, out_ref, other_ref
):
    def out_places(odd_band):
        up, down = jnp.where(odd_band == 1, 0, 2), jnp.where(odd_band == 1, 2, 0)
        return {-1: down, 0: up, 1: up + 1}

    spread(
        wanted, out_places, out_ref, words_ref, x_ref, tail_ref, units_ref, far_ref, other_ref
    )


def products(parts, field):
    high, low = split(field)
    dot = functools.partial(jnp.dot, preferred_element_type=jnp.float32)
    return dot(parts[0], high) + (dot(parts[0], low) + dot(parts[1], high))


def side_by_side(fields):
    return jnp.concatenate(fields, axis=1)


def middle_kernel(
    wanted, words_ref, x_ref, tail_ref, units_ref, far_ref, inverse_ref,
    first_ref, parts_ref, edge_ref,
    mid_ref, matrix_ref, other_ref,
):
    rows, tracers, levels, cols = first_ref.shape
    size = inverse_ref.shape[2]
    spread(wanted, None, mid_ref, words_ref, x_ref, tail_ref, units_ref, far_ref, other_ref)
    matrix_ref[...] = jnp.zeros(matrix_ref.shape, jnp.float32)
    level_of = lax.broadcasted_iota(jnp.int32, (levels, 1), 0)
    for i in range(rows):
        matrix_ref[0:size, 0:size] = inverse_ref[i, 0]
        matrix_ref[size:levels, size:levels] = inverse_ref[i, 1]
        matrix = matrix_ref[...]
        parts = split(matrix)
        parts_ref[i, 0] = parts[0]
        parts_ref[i, 1] = parts[1]
        edge = jnp.where(level_of < size, matrix[0:levels, size - 1 : size], matrix[0:levels, size : size + 1])
        edge_ref[i] = jnp.broadcast_to(edge, (levels, cols))
        first = products(parts, side_by_side([mid_ref[i, t * levels : (t + 1) * levels, :] for t in range(tracers)]))
        for t in range(tracers):
            first_ref[i, t] = first[0:levels, t * cols : (t + 1) * cols]


def finish_kernel(words_ref, tail_ref, first_ref, parts_ref, edge_ref, cross_ref, chip_ref, out_hbm, out_ref, sems):
    rows, tracers, levels, cols = first_ref.shape
    size = levels // 2
    odd_band = words_ref[1:2, :] == 1
    level_of = lax.broadcasted_iota(jnp.int32, (levels, cols), 0)
    copies = []
    for i in sorted(range(rows), key=lambda i: i < 2 or i == rows - 1):
        parts = [parts_ref[i, 0], parts_ref[i, 1]]
        coupling = tail_ref[i, 2:3, :]
        rims = []
        if i < 2:
            rims.append([jnp.where(odd_band, chip_ref[i, t], cross_ref[i, t]) for t in range(tracers)])
        if i == rows - 1:
            rims.append([jnp.where(odd_band, cross_ref[0, t], chip_ref[0, t]) for t in range(tracers)])
        added = [products(parts, side_by_side(rim)) for rim in rims]
        for t in range(tracers):
            first = first_ref[i, t]
            for part in added:
                first = first + part[0:levels, t * cols : (t + 1) * cols]
            other = jnp.where(
                level_of < size, coupling * first[size : size + 1, :], coupling * first[size - 1 : size, :]
            )
            out_ref[i, t] = first + edge_ref[i] * other
            copies.append(pltpu.make_async_copy(out_ref.at[i, t], out_hbm.at[i, t], sems.at[i, t]))
            copies[-1].start()
    for copy in copies:
        copy.wait()


def on_device(adjoint_in, frac_x, frac_y, dep_tile, dep_col, block_inverse, coupling):
    rows, tracers, levels, cols = adjoint_in.shape
    flat = tracers * levels
    half = (flat + 2 + 2 * PIECE - 1) // (2 * PIECE) * PIECE
    most = 2 * rows
    room = most + 4
    x = adjoint_in.reshape(rows, flat, cols)
    f32 = jnp.float32
    vmem = pl.BlockSpec(memory_space=pltpu.VMEM)
    smem = pl.BlockSpec(memory_space=pltpu.SMEM)
    params = pltpu.CompilerParams(vmem_limit_bytes=VMEM_BYTES)

    units, far, tail, words, index = pl.pallas_call(
        pack_kernel,
        name="pack",
        out_shape=(
            jax.ShapeDtypeStruct((2 * room, half, cols), f32),
            jax.ShapeDtypeStruct((2, 2 * PIECE, cols), f32),
            jax.ShapeDtypeStruct((rows, PIECE, cols), f32),
            jax.ShapeDtypeStruct((PIECE, cols), jnp.int32),
            jax.ShapeDtypeStruct((1,), jnp.int32),
        ),
        in_specs=[pl.BlockSpec(memory_space=pltpu.HBM)] * 6,
        out_specs=(vmem, vmem, vmem, vmem, smem),
        scratch_shapes=[
            pltpu.SMEM((rows,), jnp.int32),
            pltpu.SMEM((rows,), jnp.int32),
            pltpu.VMEM((rows, flat, cols), f32),
            pltpu.VMEM((rows, cols), f32),
            pltpu.VMEM((rows, cols), f32),
            pltpu.VMEM((rows, cols), f32),
            pltpu.SemaphoreType.DMA((5,)),
            pltpu.SemaphoreType.DMA((rows,)),
        ],
        compiler_params=pltpu.CompilerParams(vmem_limit_bytes=PACK_BYTES),
    )(dep_tile, dep_col, x, frac_x, frac_y, coupling)

    def exchange(right_units, left_units):
        def run(units, far):
            sends, places = [], []
            if right_units:
                sends.append((units[:right_units], 1))
                places.append((0, 0, 0))
            if left_units:
                sends.append((units[room : room + left_units], -1))
                places.append((room, 0, 0))
            if left_units > right_units:
                sends.reverse()
                places.reverse()
            sends.append((far[0], 2))
            sends.append((far[1], -2))
            taken = lax.optimization_barrier(tuple(value for value, _ in sends))
            arrived = [passed_along(value, "lon", by) for value, (_, by) in zip(taken, sends)]
            arrived = lax.optimization_barrier(tuple(arrived))
            for place, value in zip(places, arrived):
                units = lax.dynamic_update_slice(units, value, place)
            far = lax.dynamic_update_slice(far, arrived[-2][None], (0, 0, 0))
            far = lax.dynamic_update_slice(far, arrived[-1][None], (1, 0, 0))
            return lax.optimization_barrier((units, far))

        return run

    sizes = [(r, both - r) for both in range(LEAST, most) for r in range(both + 1)]
    sizes += [(r, most + 1 - r) for r in range(1, most + 1)]
    branches = [exchange(r, l) for r, l in sizes]
    units, far = lax.switch(index[0], branches, units, far)

    rim, middle = [], []
    for i in range(rows):
        for a in range(4):
            t = i + a - 1
            if t < 0:
                rim.append((i, a, t))
            elif t >= rows:
                rim.append((i, a, t - rows))
            else:
                middle.append((i, a, t))
    others = [pltpu.VMEM((2 * half, cols), f32)]
    operands = (words, x, tail, units, far)
    out = pl.pallas_call(
        functools.partial(rim_kernel, rim),
        name="rim",
        out_shape=jax.ShapeDtypeStruct((4, flat, cols), f32),
        in_specs=[vmem] * 5,
        out_specs=vmem,
        scratch_shapes=others,
        compiler_params=params,
    )(*operands)
    cross = swapped(out[:2], "lat", 1)
    chip = swapped(out[2:], "lat", 0)
    tall = (levels + 15) // 16 * 16
    first, parts, edge = pl.pallas_call(
        functools.partial(middle_kernel, middle),
        name="middle",
        out_shape=(
            jax.ShapeDtypeStruct(adjoint_in.shape, f32),
            jax.ShapeDtypeStruct((rows, 2, tall, levels), jnp.bfloat16),
            jax.ShapeDtypeStruct((rows, levels, cols), f32),
        ),
        in_specs=[vmem] * 6,
        out_specs=(vmem,) * 3,
        scratch_shapes=[pltpu.VMEM((rows, flat, cols), f32), pltpu.VMEM((tall, levels), f32)] + others,
        compiler_params=params,
    )(*operands, block_inverse)
    return pl.pallas_call(
        finish_kernel,
        name="finish",
        out_shape=jax.ShapeDtypeStruct(adjoint_in.shape, f32),
        in_specs=[vmem] * 7,
        out_specs=pl.BlockSpec(memory_space=pltpu.HBM),
        scratch_shapes=[pltpu.VMEM(adjoint_in.shape, f32), pltpu.SemaphoreType.DMA((rows, tracers))],
        compiler_params=params,
    )(
        words, tail, first, parts, edge,
        cross.reshape(2, tracers, levels, cols), chip.reshape(2, tracers, levels, cols),
    )


def solution(mesh):
    return jax.shard_map(
        on_device,
        mesh=mesh,
        in_specs=(
            P("lat", None, None, "lon"),
            P("lat", "lon"),
            P("lat", "lon"),
            P("lat"),
            P("lat"),
            P("lat", None, None, None),
            P("lat", "lon"),
        ),
        out_specs=P("lat", None, None, "lon"),
        check_vma=False,
    )
```

```python
import functools

import jax
import jax.numpy as jnp
from jax import lax
from jax.experimental import pallas as pl
from jax.experimental.pallas import tpu as pltpu
from jax.sharding import PartitionSpec as P

PIECE = 8
LEAST = 3
VMEM_BYTES = 48 * 1024 * 1024
PACK_BYTES = 63700992


def passed_along(x, axis, by):
    devices = lax.axis_size(axis)
    return lax.ppermute(x, axis, [(i, (i + by) % devices) for i in range(devices)])


def swapped(x, axis, first):
    devices = lax.axis_size(axis)
    pairs = [(i, i + 1) for i in range(first, devices - 1, 2)]
    return lax.ppermute(x, axis, pairs + [(j, i) for i, j in pairs])


def wx_weights(f):
    return [
        -f * (f - 1.0) * (f - 2.0) / 6.0,
        (f + 1.0) * (f - 1.0) * (f - 2.0) / 2.0,
        -(f + 1.0) * f * (f - 2.0) / 2.0,
        (f + 1.0) * f * (f - 1.0) / 6.0,
    ]


def plan(offsets, cols):
    right_at, left_at = jnp.int32(0), jnp.int32(0)
    entries = []
    for s in offsets:
        right_w = jnp.where(s >= 0, jnp.minimum(s + 2, cols), jnp.where(s == -1, 1, 0))
        left_w = jnp.where(s < 0, jnp.minimum(1 - s, cols), jnp.where(s == 0, 1, 0))
        entries.append((s, right_at, right_w, left_at, left_w))
        right_at = right_at + right_w
        left_at = left_at + left_w
    return entries, right_at, left_at


def read_offsets(words_ref, rows, cols):
    words = [words_ref[0, k] for k in range((rows + 3) // 4)]
    return [
        jnp.bitwise_and(lax.shift_right_logical(words[i // 4], 8 * (i % 4)), 2 * cols - 1) - cols
        for i in range(rows)
    ]


def any_of(flags):
    result = flags[0]
    for flag in flags[1:]:
        result = result | flag
    return result


def pack_kernel(
    tile_hbm, col_hbm, x_hbm, fx_hbm, fy_hbm, coupling_hbm,
    units_ref, far_ref, tail_ref, words_ref, index_ref,
    tile_ref, col_ref, x_ref, fx_ref, fy_ref, coupling_ref, small_sems, row_sems,
):
    rows, levels, cols = x_ref.shape
    half = units_ref.shape[1]
    unit = cols // 2
    most = 2 * rows
    room = units_ref.shape[0] // 2
    small = [
        pltpu.make_async_copy(src, dst, small_sems.at[k])
        for k, (src, dst) in enumerate(
            [
                (tile_hbm, tile_ref),
                (col_hbm, col_ref),
                (fx_hbm, fx_ref),
                (fy_hbm, fy_ref),
                (coupling_hbm, coupling_ref),
            ]
        )
    ]
    for copy in small:
        copy.start()
    big = [pltpu.make_async_copy(x_hbm.at[i], x_ref.at[i], row_sems.at[i]) for i in range(rows)]
    for copy in big:
        copy.start()
    for copy in small:
        copy.wait()
    offsets = [tile_ref[i] * cols + col_ref[i] for i in range(rows)]
    entries, right_total, left_total = plan(offsets, cols)
    r = (right_total + unit - 1) // unit
    l = (left_total + unit - 1) // unit
    l = l + jnp.maximum(LEAST - r - l, 0)
    full = r + l == most
    r = jnp.where(full & (l == most), r + 1, r)
    l = jnp.where(full & (l < most), l + 1, l)
    both = r + l
    before = jnp.where(both > most, most * (most + 1) // 2 - 1, both * (both + 1) // 2)
    index_ref[0] = before - LEAST * (LEAST + 1) // 2 + r

    lane = lax.broadcasted_iota(jnp.int32, (PIECE, cols), 1)
    low_lane = jnp.bitwise_and(lane, unit - 1)
    low_half = lane < unit
    sub = lax.broadcasted_iota(jnp.int32, (PIECE, cols), 0)
    words = jnp.zeros((PIECE, cols), jnp.int32)
    for k in range((rows + 3) // 4):
        word = jnp.int32(0)
        for i in range(4 * k, min(4 * k + 4, rows)):
            word = word | lax.shift_left(offsets[i] + cols, 8 * (i % 4))
        words = jnp.where(lane == k, word, words)
    odd_band = jnp.bitwise_and(lax.axis_index("lat"), 1)
    words_ref[...] = jnp.where(sub == 1, odd_band, words)
    for i in range(rows):
        tail_ref[i] = jnp.where(
            sub == 0, fx_ref[i : i + 1, :], jnp.where(sub == 1, fy_ref[i : i + 1, :], coupling_ref[i : i + 1, :])
        )

    def place(i, base, start, at, width):
        shift = jnp.bitwise_and(at - start, cols - 1)
        window = at // cols
        masks = []
        for k in range(4):
            place_of = (2 * window + k) * unit + low_lane
            masks.append((place_of >= at) & (place_of < at + width))
        for level in range(0, half, PIECE):
            lo = x_ref[i, level : level + PIECE, :]
            hi = x_ref[i, half + level : half + level + PIECE, :] if half + level < levels else tail_ref[i]
            lo = pltpu.roll(lo, shift, 1)
            hi = pltpu.roll(hi, shift, 1)
            even = jnp.where(low_half, lo, pltpu.roll(hi, unit, 1))
            odd = jnp.where(low_half, pltpu.roll(lo, unit, 1), hi)
            for k in range(4):
                u = base + 2 * window + k
                old = units_ref[u, level : level + PIECE, :]
                units_ref[u, level : level + PIECE, :] = jnp.where(masks[k], odd if k % 2 else even, old)

    for i in range(rows):
        s, right_at, right_w, left_at, left_w = entries[i]
        goes_right = s >= 0
        big[i].wait()
        place(
            i,
            jnp.where(goes_right, 0, room),
            jnp.where(goes_right, cols - right_w, 0),
            jnp.where(goes_right, right_at, left_at),
            jnp.where(goes_right, right_w, left_w),
        )

    def place_far(i, which, column):
        for k in range(2):
            block = far_ref[which, k * PIECE : (k + 1) * PIECE, :]
            for f in range(half // PIECE):
                level = (2 * f + k) * PIECE
                value = x_ref[i, level : level + PIECE, :] if level < levels else tail_ref[i]
                to = rows * f + i
                block = jnp.where(lane == to, pltpu.roll(value, (to - column) % cols, 1), block)
            far_ref[which, k * PIECE : (k + 1) * PIECE, :] = block

    @pl.when(any_of([(s == 0) | (s == -1) | (s == cols - 1) | (s == -cols) for s in offsets]))
    def _():
        for i in range(rows):
            s, right_at, right_w, left_at, left_w = entries[i]

            @pl.when((s == 0) | (s == -1))
            def _():
                zero = s == 0
                place(
                    i, jnp.where(zero, room, 0), jnp.where(zero, 0, cols - 1), jnp.where(zero, left_at, right_at), 1
                )

            @pl.when(s == cols - 1)
            def _():
                place_far(i, 0, cols - 1)

            @pl.when(s == -cols)
            def _():
                place_far(i, 1, 0)


def split(value):
    high = value.astype(jnp.bfloat16)
    return high, (value - high.astype(jnp.float32)).astype(jnp.bfloat16)


def dot_nt(left, right):
    return lax.dot_general(left, right, (((1,), (1,)), ((), ())), preferred_element_type=jnp.float32)


def spread(wanted, out_places, out_ref, words_ref, x_ref, tail_ref, units_ref, far_ref, other_ref):
    rows, levels, cols = x_ref.shape
    half = units_ref.shape[1]
    unit = cols // 2
    room = units_ref.shape[0] // 2
    offsets = read_offsets(words_ref, rows, cols)
    entries, _, _ = plan(offsets, cols)
    lane = lax.broadcasted_iota(jnp.int32, (1, cols), 1)
    low_lane = jnp.bitwise_and(lane, unit - 1)
    low_half = lane < unit
    to = lax.broadcasted_iota(jnp.int32, (cols, cols), 0)
    chosen = sorted({w[0] for w in wanted})
    seen = set()
    at_of = out_places(words_ref[1, 0]) if out_places else {w[2]: w[2] for w in wanted}

    def matrices(fractions, column, which):
        b_of = to - column + 1
        wx = wx_weights(fractions[0:1, :])
        wy = wx_weights(fractions[1:2, :])
        along = jnp.where(b_of == 0, wx[0], 0.0)
        for b in range(1, 4):
            along = jnp.where(b_of == b, wx[b], along)
        return [split(along * wy[a]) for a in which]

    for i in chosen:
        mine = [w[1:] for w in wanted if w[0] == i]
        which = [a for a, _ in mine]
        s, right_at, right_w, left_at, left_w = entries[i]
        goes_right = s >= 0
        at = jnp.where(goes_right, right_at, left_at)
        width = jnp.where(goes_right, right_w, left_w)
        base = jnp.where(goes_right, 0, room) + 2 * (at // cols)
        om = jnp.bitwise_and(at, cols - 1)
        place = jnp.bitwise_and(lane - at, cols - 1)
        held = place < width
        start = jnp.where(goes_right, s - width, s + cols)

        piece = [units_ref[base + k] for k in range(4)]
        even = jnp.where(low_lane >= om, piece[0], piece[2])
        odd = jnp.where(low_lane + unit >= om, piece[1], piece[3])
        got = [
            jnp.where(held, jnp.where(low_half, even, pltpu.roll(odd, unit, 1)), 0.0),
            jnp.where(held, jnp.where(low_half, pltpu.roll(even, unit, 1), odd), 0.0),
        ]
        home = [
            x_ref[i, 0:half, :],
            jnp.concatenate([x_ref[i, half:levels, :], jnp.zeros((2 * half - levels, cols), jnp.float32)], axis=0),
        ]
        from_home = matrices(tail_ref[i], lane + s, which)
        from_got = matrices(got[1][half - PIECE : half, :], jnp.where(held, start + place, -2 * cols), which)
        ones = [
            jnp.concatenate([jnp.concatenate([h[part], g[part]], axis=1) for h, g in zip(from_home, from_got)], axis=0)
            for part in range(2)
        ]
        for p in range(2):
            home_parts, got_parts = split(home[p]), split(got[p])
            high, low = [jnp.concatenate([home_parts[part], got_parts[part]], axis=1) for part in range(2)]
            total = dot_nt(high, ones[0]) + (dot_nt(high, ones[1]) + dot_nt(low, ones[0]))
            size = half if p == 0 else levels - half
            for n, (a, k) in enumerate(mine):
                value = total[0:size, n * cols : (n + 1) * cols]
                if k in seen:
                    value = value + out_ref[at_of[k], p * half : p * half + size, :]
                out_ref[at_of[k], p * half : p * half + size, :] = value
        seen.update(k for _, k in mine)

    def add_other(i, lane_to, b):
        fractions = other_ref[2 * half - PIECE : 2 * half, :]
        wx = wx_weights(fractions[0:1, :])[b]
        wy = wx_weights(fractions[1:2, :])
        for row, a, k in wanted:
            if row == i:
                weight = wx * wy[a]
                for level in range(0, levels, PIECE):
                    old = out_ref[at_of[k], level : level + PIECE, :]
                    new = old + other_ref[level : level + PIECE, :] * weight
                    out_ref[at_of[k], level : level + PIECE, :] = jnp.where(lane == lane_to, new, old)

    def fetch_unit(u, place, lane_to):
        for level in range(0, half, PIECE):
            value = units_ref[u, level : level + PIECE, :]
            other_ref[level : level + PIECE, :] = pltpu.roll(value, jnp.bitwise_and(lane_to - place, cols - 1), 1)
            other_ref[half + level : half + level + PIECE, :] = pltpu.roll(
                value, jnp.bitwise_and(lane_to - place - unit, cols - 1), 1
            )

    def fetch_far(i, which, lane_to):
        for k in range(2):
            block = far_ref[which, k * PIECE : (k + 1) * PIECE, :]
            for f in range(half // PIECE):
                level = (2 * f + k) * PIECE
                other_ref[level : level + PIECE, :] = pltpu.roll(block, (lane_to - rows * f - i) % cols, 1)

    @pl.when(any_of([(s == 0) | (s == -1) | (s == cols - 1) | (s == -cols) for s in (offsets[i] for i in chosen)]))
    def _():
        for i in chosen:
            s, right_at, right_w, left_at, left_w = entries[i]

            @pl.when(s == 0)
            def _():
                fetch_unit(room + left_at // unit, jnp.bitwise_and(left_at, unit - 1), cols - 1)
                add_other(i, cols - 1, 0)

            @pl.when(s == -1)
            def _():
                fetch_unit(right_at // unit, jnp.bitwise_and(right_at, unit - 1), 0)
                add_other(i, 0, 3)

            @pl.when(s == cols - 1)
            def _():
                fetch_far(i, 0, 0)
                add_other(i, 0, 3)

            @pl.when(s == -cols)
            def _():
                fetch_far(i, 1, cols - 1)
                add_other(i, cols - 1, 0)


def rim_kernel(
    wanted, words_ref, x_ref, tail_ref, units_ref, far_ref, out_ref, other_ref
):
    def out_places(odd_band):
        up, down = jnp.where(odd_band == 1, 0, 2), jnp.where(odd_band == 1, 2, 0)
        return {-1: down, 0: up, 1: up + 1}

    spread(
        wanted, out_places, out_ref, words_ref, x_ref, tail_ref, units_ref, far_ref, other_ref
    )


def products(parts, field):
    high, low = split(field)
    dot = functools.partial(jnp.dot, preferred_element_type=jnp.float32)
    return dot(parts[0], high) + (dot(parts[0], low) + dot(parts[1], high))


def side_by_side(fields):
    return jnp.concatenate(fields, axis=1)


def middle_kernel(
    wanted, words_ref, x_ref, tail_ref, units_ref, far_ref, inverse_ref,
    first_ref, parts_ref, edge_ref,
    mid_ref, matrix_ref, other_ref,
):
    rows, tracers, levels, cols = first_ref.shape
    size = inverse_ref.shape[2]
    spread(wanted, None, mid_ref, words_ref, x_ref, tail_ref, units_ref, far_ref, other_ref)
    matrix_ref[...] = jnp.zeros(matrix_ref.shape, jnp.float32)
    level_of = lax.broadcasted_iota(jnp.int32, (levels, 1), 0)
    for i in range(rows):
        matrix_ref[0:size, 0:size] = inverse_ref[i, 0]
        matrix_ref[size:levels, size:levels] = inverse_ref[i, 1]
        matrix = matrix_ref[...]
        parts = split(matrix)
        parts_ref[i, 0] = parts[0]
        parts_ref[i, 1] = parts[1]
        edge = jnp.where(level_of < size, matrix[0:levels, size - 1 : size], matrix[0:levels, size : size + 1])
        edge_ref[i] = jnp.broadcast_to(edge, (levels, cols))
        first = products(parts, side_by_side([mid_ref[i, t * levels : (t + 1) * levels, :] for t in range(tracers)]))
        for t in range(tracers):
            first_ref[i, t] = first[0:levels, t * cols : (t + 1) * cols]


def finish_kernel(words_ref, tail_ref, first_ref, parts_ref, edge_ref, cross_ref, chip_ref, out_hbm, out_ref, sems):
    rows, tracers, levels, cols = first_ref.shape
    size = levels // 2
    odd_band = words_ref[1:2, :] == 1
    level_of = lax.broadcasted_iota(jnp.int32, (levels, cols), 0)
    copies = []
    for i in sorted(range(rows), key=lambda i: i < 2 or i == rows - 1):
        parts = [parts_ref[i, 0], parts_ref[i, 1]]
        coupling = tail_ref[i, 2:3, :]
        rims = []
        if i < 2:
            rims.append([jnp.where(odd_band, chip_ref[i, t], cross_ref[i, t]) for t in range(tracers)])
        if i == rows - 1:
            rims.append([jnp.where(odd_band, cross_ref[0, t], chip_ref[0, t]) for t in range(tracers)])
        added = [products(parts, side_by_side(rim)) for rim in rims]
        for t in range(tracers):
            first = first_ref[i, t]
            for part in added:
                first = first + part[0:levels, t * cols : (t + 1) * cols]
            other = jnp.where(
                level_of < size, coupling * first[size : size + 1, :], coupling * first[size - 1 : size, :]
            )
            out_ref[i, t] = first + edge_ref[i] * other
            copies.append(pltpu.make_async_copy(out_ref.at[i, t], out_hbm.at[i, t], sems.at[i, t]))
            copies[-1].start()
    for copy in copies:
        copy.wait()


def on_device(adjoint_in, frac_x, frac_y, dep_tile, dep_col, block_inverse, coupling):
    rows, tracers, levels, cols = adjoint_in.shape
    flat = tracers * levels
    half = (flat + 2 + 2 * PIECE - 1) // (2 * PIECE) * PIECE
    most = 2 * rows
    room = most + 4
    x = adjoint_in.reshape(rows, flat, cols)
    f32 = jnp.float32
    vmem = pl.BlockSpec(memory_space=pltpu.VMEM)
    smem = pl.BlockSpec(memory_space=pltpu.SMEM)
    params = pltpu.CompilerParams(vmem_limit_bytes=VMEM_BYTES)

    units, far, tail, words, index = pl.pallas_call(
        pack_kernel,
        name="pack",
        out_shape=(
            jax.ShapeDtypeStruct((2 * room, half, cols), f32),
            jax.ShapeDtypeStruct((2, 2 * PIECE, cols), f32),
            jax.ShapeDtypeStruct((rows, PIECE, cols), f32),
            jax.ShapeDtypeStruct((PIECE, cols), jnp.int32),
            jax.ShapeDtypeStruct((1,), jnp.int32),
        ),
        in_specs=[pl.BlockSpec(memory_space=pltpu.HBM)] * 6,
        out_specs=(vmem, vmem, vmem, vmem, smem),
        scratch_shapes=[
            pltpu.SMEM((rows,), jnp.int32),
            pltpu.SMEM((rows,), jnp.int32),
            pltpu.VMEM((rows, flat, cols), f32),
            pltpu.VMEM((rows, cols), f32),
            pltpu.VMEM((rows, cols), f32),
            pltpu.VMEM((rows, cols), f32),
            pltpu.SemaphoreType.DMA((5,)),
            pltpu.SemaphoreType.DMA((rows,)),
        ],
        compiler_params=pltpu.CompilerParams(vmem_limit_bytes=PACK_BYTES),
    )(dep_tile, dep_col, x, frac_x, frac_y, coupling)

    def exchange(right_units, left_units):
        def run(units, far):
            sends, places = [], []
            if right_units:
                sends.append((units[:right_units], 1))
                places.append((0, 0, 0))
            if left_units:
                sends.append((units[room : room + left_units], -1))
                places.append((room, 0, 0))
            if left_units > right_units:
                sends.reverse()
                places.reverse()
            sends.append((far[0], 2))
            sends.append((far[1], -2))
            taken = lax.optimization_barrier(tuple(value for value, _ in sends))
            arrived = [passed_along(value, "lon", by) for value, (_, by) in zip(taken, sends)]
            arrived = lax.optimization_barrier(tuple(arrived))
            for place, value in zip(places, arrived):
                units = lax.dynamic_update_slice(units, value, place)
            far = lax.dynamic_update_slice(far, arrived[-2][None], (0, 0, 0))
            far = lax.dynamic_update_slice(far, arrived[-1][None], (1, 0, 0))
            return lax.optimization_barrier((units, far))

        return run

    sizes = [(r, both - r) for both in range(LEAST, most) for r in range(both + 1)]
    sizes += [(r, most + 1 - r) for r in range(1, most + 1)]
    branches = [exchange(r, l) for r, l in sizes]
    units, far = lax.switch(index[0], branches, units, far)

    rim, middle = [], []
    for i in range(rows):
        for a in range(4):
            t = i + a - 1
            if t < 0:
                rim.append((i, a, t))
            elif t >= rows:
                rim.append((i, a, t - rows))
            else:
                middle.append((i, a, t))
    others = [pltpu.VMEM((2 * half, cols), f32)]
    operands = (words, x, tail, units, far)
    out = pl.pallas_call(
        functools.partial(rim_kernel, rim),
        name="rim",
        out_shape=jax.ShapeDtypeStruct((4, flat, cols), f32),
        in_specs=[vmem] * 5,
        out_specs=vmem,
        scratch_shapes=others,
        compiler_params=params,
    )(*operands)
    cross = swapped(out[:2], "lat", 1)
    chip = swapped(out[2:], "lat", 0)
    tall = (levels + 15) // 16 * 16
    first, parts, edge = pl.pallas_call(
        functools.partial(middle_kernel, middle),
        name="middle",
        out_shape=(
            jax.ShapeDtypeStruct(adjoint_in.shape, f32),
            jax.ShapeDtypeStruct((rows, 2, tall, levels), jnp.bfloat16),
            jax.ShapeDtypeStruct((rows, levels, cols), f32),
        ),
        in_specs=[vmem] * 6,
        out_specs=(vmem,) * 3,
        scratch_shapes=[pltpu.VMEM((rows, flat, cols), f32), pltpu.VMEM((tall, levels), f32)] + others,
        compiler_params=params,
    )(*operands, block_inverse)
    return pl.pallas_call(
        finish_kernel,
        name="finish",
        out_shape=jax.ShapeDtypeStruct(adjoint_in.shape, f32),
        in_specs=[vmem] * 7,
        out_specs=pl.BlockSpec(memory_space=pltpu.HBM),
        scratch_shapes=[pltpu.VMEM(adjoint_in.shape, f32), pltpu.SemaphoreType.DMA((rows, tracers))],
        compiler_params=params,
    )(
        words, tail, first, parts, edge,
        cross.reshape(2, tracers, levels, cols), chip.reshape(2, tracers, levels, cols),
    )


def solution(mesh):
    return jax.shard_map(
        on_device,
        mesh=mesh,
        in_specs=(
            P("lat", None, None, "lon"),
            P("lat", "lon"),
            P("lat", "lon"),
            P("lat"),
            P("lat"),
            P("lat", None, None, None),
            P("lat", "lon"),
        ),
        out_specs=P("lat", None, None, "lon"),
        check_vma=False,
    )
```
